256 devices in a mesh: gx: 4 (over x), gy: 4 (over z_hi, core), gz: 16 (over y, z_lo).
Axes of the slice: x: 4, y: 4, z: 8 (z_hi: 2, z_lo: 4; z = z_hi * 4 + z_lo), core: 2. Of those that a mesh axis runs over, the one named last changes fastest.
Arguments:
- adjoint: float32 [5, 16, 128, 4096], P(None, 'gx', 'gy', 'gz'), may hold values from -6 to 6
- viscosity: float32 [16, 128, 4096], P('gx', 'gy', 'gz'), may hold values from 0.5 to 2
- flux_jacobian: float32 [5, 5], replicated, may hold values from -4 to 4
- face_cell: int32 [262144], P(('gx', 'gy', 'gz')), may hold values from 0 to 32767
- face_patch: int32 [262144, 1], P(('gx', 'gy', 'gz')), may hold values from 0 to 15; in each aligned block of 1024 rows (0 to 1023, 1024 to 2047, ...) at most 128 rows name the same one
- wall_inverse: float32 [256, 128, 128], P(('gx', 'gy', 'gz')), may hold values from -1.2 to 1.2
- lift_matrix: float32 [128, 6], replicated, may hold values from -2.5 to 2.5
- readout: float32 [5, 128], replicated, may hold values from -0.5 to 0.5
Outputs:
- updated: float32 [5, 16, 128, 4096], P(None, 'gx', 'gy', 'gz')
- wall_shear: float32 [5, 262144], P(None, ('gx', 'gy', 'gz'))
The draws below stay inside these ranges and needn't reach their ends.
Inputs may be any that keep to these rules, and one draw needn't show every extreme that they name: face_cell numbers a cell inside the block of the face's own device. `face_patch`: A patch number p of a face belongs to the device with gz index p // 1 in the face's own (gx, gy) column. Among the 1024 faces of one device at most 128 name one patch, and in every draw some patch is named by exactly 128 faces of some device.
All inputs are finite; a program needn't handle non-finite values.
Results may differ from the reference program's by a relative error of at most 0.0003.
Values sent between devices are 32-bit elements; how exact they have to be, the bound alone decides.
No kernel may reach another device: no remote copies, remote signals or barrier semaphores. Data moves between devices by JAX's collectives and lax.ppermute only.
A program may use at most 64 MiB of HBM per device.

```python
import math
import jax
import jax.numpy as jnp
import numpy as np
from jax import lax

CX = 4
CY = 32
CZ = 256
FACE_DEV = 1024
PATCH_DEV = 1
ITERS = 6
PROF = 128
NX = 16
NY = 128
NZ = 4096
FACES = 262144
PATCHES = 256
CAP = 128
N_GX = 4
N_GY = 4
N_GZ = 16
DEVICES = 256


def draw_wall_inverse(key, part):
    key = jax.random.fold_in(key, 11)
    diag_key, off_key = jax.random.split(key)
    diagonal = jax.random.uniform(diag_key, (PATCHES, PROF), jnp.float32, 0.8, 1.2)
    spread = 0.6 / PROF ** 0.5
    off_part = spread * jax.random.truncated_normal(off_key, -3.0, 3.0, (PATCHES, PROF, PROF), jnp.float32)
    identity = jnp.eye(PROF, dtype=jnp.float32)
    return off_part * (1.0 - identity) + diagonal[:, :, None] * identity


def set_ends(drawn, rng, low, top_value):
    longest = drawn.shape.index(max(drawn.shape))
    spots = []
    for shift in (0, 1):
        where = [jax.random.randint(jax.random.fold_in(rng, axis), (), 0, length) for axis, length in enumerate(drawn.shape)]
        where[longest] = (where[longest] + shift) % drawn.shape[longest]
        spots.append(tuple(where))
    return drawn.at[spots[0]].set(low).at[spots[1]].set(top_value)


def levels(stream_key, shape, pieces, least, largest):
    level, own = 1.0, jax.random.fold_in(stream_key, 6)
    for axis_at, blocks in pieces:
        heights = jnp.exp(jax.random.uniform(jax.random.fold_in(own, axis_at), (blocks,), jnp.float32, least / len(pieces), largest / len(pieces)))
        level = level * jnp.repeat(heights, shape[axis_at] // blocks).reshape([-1 if axis == axis_at else 1 for axis in range(len(shape))])
    return level


def shared_out(own_key, own, number, rows, number_of, top, bound, slope):
    ranking = jax.random.permutation(own_key, number_of)
    heavy_load, ordinary = shares(number_of, rows * top, bound, slope, True), shares(number_of, rows * top, bound, slope, False)
    places = jnp.arange(number_of)

    def named(sizes, turn):
        used = int((sizes > 0).sum())
        fixed = max(1, used // 4)
        passed = fixed + (places - fixed + turn * (used - fixed)) % max(1, number_of - fixed)
        return jnp.zeros((number_of,), jnp.int32).at[ranking[jnp.where(places < fixed, places, passed)]].set(jnp.asarray(sizes, jnp.int32))

    sizes = jnp.where(number % 4 == 0, named(heavy_load, number // 4), named(ordinary, number - number // 4 - 1))
    mixed = jax.random.permutation(jax.random.fold_in(own, 3), number_of)
    source_of, sink = mixed[0:number_of // 2 * 2:2], mixed[1:number_of // 2 * 2:2]
    slack = jnp.minimum(sizes[source_of] - 1, bound - sizes[sink]) // 2
    slack = jnp.where((source_of == ranking[0]) | (sink == ranking[0]) | (sizes[sink] == 0), 0, jnp.maximum(slack, 0))
    passed = jax.random.randint(jax.random.fold_in(own, 4), (number_of // 2,), 0, 1 << 20) % (slack + 1)
    sizes = sizes.at[source_of].add(-passed).at[sink].add(passed)
    items = jnp.searchsorted(jnp.cumsum(sizes), jnp.arange(rows * top), side="right").astype(jnp.int32)
    listing = items.reshape(top, rows).T
    listing = listing[jax.random.permutation(jax.random.fold_in(own, 1), rows)]
    turn = jax.random.randint(jax.random.fold_in(own, 2), (rows, 1), 0, top)
    return jnp.take_along_axis(listing, (jnp.arange(top)[None, :] + turn) % top, axis=1)


def shares(amount, total, bound, skew, full):
    weights = [(1 << 20) // math.isqrt(grade ** skew) + 1 for grade in range(1, amount + 1)]
    largest = bound if full else min(bound, max(-(-total // amount), total * weights[0] // sum(weights)))
    least = 1 if total - largest >= amount - 1 else 0
    holding, spare = [largest] + [least] * (amount - 1), total - largest - least * (amount - 1)
    while spare > 0:
        candidates = [i for i in range(1, amount) if holding[i] < largest] or [i for i in range(1, amount) if holding[i] < bound]
        pool, budget = sum([weights[i] for i in candidates]), spare
        for i in candidates:
            extra = min(bound - holding[i], max(1, budget * weights[i] // pool), spare)
            holding[i] = holding[i] + extra
            spare = spare - extra
    return np.array(holding)


def scatter_about(own_key, extent, deviation, most, shards=(), kind=jnp.bfloat16):
    loudness = levels(own_key, extent, shards, -0.22, 0.18) if shards else 1.0
    drawn = jax.random.normal(own_key, extent, jnp.float32) * deviation * loudness
    return jnp.minimum(jnp.maximum(drawn, -most), most).astype(kind)


def setup_inputs(seed: int = 0) -> dict:
    splits = jax.random.split(jax.random.key(seed), 9)
    adjoint = scatter_about(splits[0], (5, NX, NY, NZ), 1.0, 6.0, ((1, 4), (2, 4), (3, 16)), jnp.float32)
    viscosity = jnp.clip(jnp.exp(math.log(2.0) - 1.3862944 * jax.random.uniform(splits[1], (NX, NY, NZ), jnp.float32) ** levels(splits[1], (NX, NY, NZ), ((0, 4), (1, 4), (2, 16)), -0.2, 0.2)), 0.5, 2.0)
    flux_jacobian = scatter_about(splits[2], (5, 5), 1.0, 4.0, (), jnp.float32)
    face_cell = set_ends(jax.random.randint(splits[3], (FACES,), 0, CX * CY * CZ), jax.random.fold_in(splits[3], 1), 0, (CX * CY * CZ) - 1).astype(jnp.int32)
    face_patch_keys = jax.random.split(jax.random.fold_in(splits[4], 1), FACES // FACE_DEV)
    face_patch_turns = jax.random.permutation(jax.random.fold_in(splits[4], 3), FACES // FACE_DEV)
    face_patch = jax.vmap(lambda own, number: shared_out(jax.random.fold_in(splits[4], 2), own, number, FACE_DEV, N_GZ * PATCH_DEV, 1, CAP, 2))(face_patch_keys, face_patch_turns).reshape((FACES, 1))
    wall_inverse = draw_wall_inverse(jax.random.fold_in(splits[8], 71), 0)
    lift_matrix = scatter_about(splits[6], (PROF, 6), 6 ** -0.5, 2.5, (), jnp.float32)
    readout = scatter_about(splits[7], (5, PROF), PROF ** -0.5, 0.5, (), jnp.float32)
    return {"adjoint": adjoint, "viscosity": viscosity, "flux_jacobian": flux_jacobian, "face_cell": face_cell, "face_patch": face_patch, "wall_inverse": wall_inverse, "lift_matrix": lift_matrix, "readout": readout}


time_step = 0.08


def solve_block(inverse, slot_rows, lift_matrix, readout):
    forcing = jnp.einsum('ic,bpcm->bpim', lift_matrix, slot_rows, precision=lax.Precision.HIGHEST)
    damping = 0.5 * slot_rows[:, :, 5:6, :]
    profile = jnp.zeros_like(forcing)
    for sweep in range(ITERS):
        profile = jnp.einsum('pij,bpjm->bpim', inverse, forcing - damping * jnp.tanh(profile), precision=lax.Precision.HIGHEST)
    return jnp.einsum('fi,bpim->bpfm', readout, profile, precision=lax.Precision.HIGHEST)


def slot_ranks(patches, patch_total):
    onehot = (patches[:, None] == jnp.arange(patch_total, dtype=jnp.int32)[None, :]).astype(jnp.int32)
    return (jnp.sum(jnp.cumsum(onehot, axis=0) * onehot, axis=1) - 1).astype(jnp.int32)


def advance(padded, source, flux_jacobian):
    center = padded[:, 1:-1, 1:-1, 1:-1]
    fields = center[:5]
    local_visc = center[5]
    neighbours = (padded[:, 2:, 1:-1, 1:-1], padded[:, :-2, 1:-1, 1:-1],
                  padded[:, 1:-1, 2:, 1:-1], padded[:, 1:-1, :-2, 1:-1],
                  padded[:, 1:-1, 1:-1, 2:], padded[:, 1:-1, 1:-1, :-2])
    diffusion = jnp.zeros_like(fields)
    for beside in neighbours:
        diffusion = diffusion + 0.5 * (local_visc + beside[5]) * (beside[:5] - fields)
    coupling = jnp.einsum('fg,gxyz->fxyz', flux_jacobian, fields, precision=lax.Precision.HIGHEST)
    return fields + time_step * (diffusion + coupling + source)


def reference(adjoint, viscosity, flux_jacobian, face_cell, face_patch, wall_inverse, lift_matrix, readout):
    cells = CX * CY * CZ
    patch_col = N_GZ * PATCH_DEV
    capacity = 2 * FACE_DEV // patch_col
    stacked = jnp.concatenate([adjoint, viscosity[None]], axis=0)
    blocks = stacked.reshape(6, N_GX, CX, N_GY, CY, N_GZ, CZ).transpose(1, 3, 5, 0, 2, 4, 6).reshape(DEVICES, 6, cells)
    cell_ids = face_cell.reshape(DEVICES, FACE_DEV)
    patch_ids = face_patch.reshape(DEVICES, FACE_DEV)
    inverses = wall_inverse.reshape(N_GX * N_GY, patch_col, PROF, PROF)

    def one_device(device):
        local = blocks[device]
        owned = cell_ids[device]
        patches = patch_ids[device]
        row_data = jnp.take(local, owned, axis=1)
        ranks = slot_ranks(patches, patch_col)
        buffer = jnp.zeros((patch_col, 6, capacity), jnp.float32).at[patches, :, ranks].set(row_data.T)
        result = solve_block(inverses[device // N_GZ], buffer[None], lift_matrix, readout)[0]
        shear = result[patches, :, ranks].T
        source = jnp.zeros((5, cells), jnp.float32).at[:, owned].add(shear)
        return shear, source

    shear_all, source_all = lax.map(one_device, jnp.arange(DEVICES, dtype=jnp.int32))
    source = source_all.reshape(N_GX, N_GY, N_GZ, 5, CX, CY, CZ).transpose(3, 0, 4, 1, 5, 2, 6).reshape(5, NX, NY, NZ)
    padded = jnp.pad(stacked, ((0, 0), (1, 1), (1, 1), (0, 0)))
    padded = jnp.concatenate([padded[..., -1:], padded, padded[..., :1]], axis=3)
    updated = advance(padded, source, flux_jacobian)
    return updated, shear_all.transpose(1, 0, 2).reshape(5, FACES)
```

```python
import functools

import jax
import jax.numpy as jnp
from jax import lax
from jax.experimental import pallas as pl
from jax.experimental.pallas import tpu as pltpu
from jax.sharding import PartitionSpec as P

CX = 4
CY = 32
CZ = 256
FACES = 1024
ROWS = CX * CY
PATCHES = 16
CAP = 128
PROF = 128
ITERS = 6
GROUP = 4

time_step = 0.08

F32 = jnp.float32
BF16 = jnp.bfloat16
VMEM = pl.BlockSpec(memory_space=pltpu.VMEM)
SMEM = pl.BlockSpec(memory_space=pltpu.SMEM)
PARAMS = pltpu.CompilerParams(vmem_limit_bytes=48 * 1024 * 1024)


def split(x):
    high = x.astype(BF16)
    low = (x - high.astype(F32)).astype(BF16)
    return high, low


def dot(a, b):
    return jnp.dot(a, b, preferred_element_type=F32)


def dot_t(a, b):
    return lax.dot_general(a, b, (((1,), (1,)), ((), ())), preferred_element_type=F32)


def one_hot(count, index, dtype):
    numbers = lax.broadcasted_iota(jnp.int32, (count, index.shape[-1]), 0)
    return jnp.where(numbers == index, 1.0, 0.0).astype(dtype)


def gather_kernel(
    adjoint, viscosity, cell, patch, x_low, x_high, y_low, y_high, z_low, z_high, slots, ranks
):
    for f in range(6):
        field = viscosity if f == 5 else adjoint.at[f]
        x_low[f] = field[0]
        x_high[f] = field[CX - 1]
        for x in range(CX):
            y_low[f * CX + x : f * CX + x + 1, :] = field[x, 0:1, :]
            y_high[f * CX + x : f * CX + x + 1, :] = field[x, CY - 1 : CY, :]
    cells = cell[...]
    patches = patch[...]
    row = cells >> 8
    span = cells & (CZ - 1)
    span_hot = one_hot(CZ, span, BF16)
    row_hot = lax.broadcasted_iota(jnp.int32, (ROWS, FACES), 0) == row
    ends = lax.broadcasted_iota(jnp.int32, (8, CZ), 0)
    lanes = lax.broadcasted_iota(jnp.int32, (8, CZ), 1)
    edge = jnp.where(
        ((ends == 0) & (lanes == 0)) | ((ends == 1) & (lanes == CZ - 1)), 1.0, 0.0
    ).astype(BF16)
    values = []
    for f in range(6):
        field = (viscosity[...] if f == 5 else adjoint[f]).reshape(ROWS, CZ)
        high, low = split(field)
        found = dot(high, span_hot) + dot(low, span_hot)
        values.append(jnp.sum(jnp.where(row_hot, found, 0.0), axis=0, keepdims=True))
        rest = (field - high.astype(F32) - low.astype(F32)).astype(BF16)
        outer = dot_t(edge, high) + dot_t(edge, low) + dot_t(edge, rest)
        z_low[f : f + 1, :] = outer[0:1]
        z_high[f : f + 1, :] = outer[1:2]
    z_low[6:8, :] = jnp.zeros((2, ROWS), F32)
    z_high[6:8, :] = jnp.zeros((2, ROWS), F32)

    hot = one_hot(PATCHES, patches, F32)
    pieces = FACES // 128
    stacked = jnp.concatenate([hot[:, b * 128 : (b + 1) * 128] for b in range(pieces)], axis=0)
    stacked = stacked.astype(BF16)
    upto = (
        lax.broadcasted_iota(jnp.int32, (128, 256), 0)
        <= lax.broadcasted_iota(jnp.int32, (128, 256), 1)
    )
    counts = dot(stacked, jnp.where(upto, 1.0, 0.0).astype(BF16))
    before = jnp.zeros((PATCHES, 128), F32)
    found_ranks = []
    for b in range(pieces):
        mine = slice(b * PATCHES, (b + 1) * PATCHES)
        piece = hot[:, b * 128 : (b + 1) * 128]
        found_ranks.append(
            jnp.sum(piece * (counts[mine, :128] + before), axis=0, keepdims=True) - 1.0
        )
        before = before + counts[mine, 128:]
    rank = jnp.concatenate(found_ranks, axis=1).astype(jnp.int32)
    ranks[...] = rank

    rank_hot = one_hot(CAP, rank, BF16)
    table = jnp.concatenate(values + [jnp.zeros((2, FACES), F32)], axis=0)
    high, low = split(table)
    both = jnp.concatenate([high.astype(F32), low.astype(F32)], axis=0)
    spread = jnp.concatenate(
        [jnp.where(patches == p, both, 0.0).astype(BF16) for p in range(PATCHES)], axis=0
    )
    placed = dot_t(spread, rank_hot).reshape(PATCHES, 16, CAP)
    slots[...] = placed[:, :8] + placed[:, 8:]


def stencil_kernel(
    adjoint, viscosity, jacobian, x_before, x_after, y_before, y_after, z_before, z_after, out
):
    gx, gy = lax.axis_index("gx"), lax.axis_index("gy")
    has_before_x = jnp.where(gx > 0, 1.0, 0.0)
    has_after_x = jnp.where(gx < lax.axis_size("gx") - 1, 1.0, 0.0)
    has_before_y = jnp.where(gy > 0, 1.0, 0.0)
    has_after_y = jnp.where(gy < lax.axis_size("gy") - 1, 1.0, 0.0)
    rows = lax.broadcasted_iota(jnp.int32, (CY, CZ), 0)
    lanes = lax.broadcasted_iota(jnp.int32, (CY, CZ), 1)
    z_low = jnp.transpose(z_before[...])
    z_high = jnp.transpose(z_after[...])

    def field_at(f, x):
        return viscosity[x] if f == 5 else adjoint[f, x]

    def neighbours(f, x):
        center = field_at(f, x)
        yield field_at(f, x - 1) if x > 0 else x_before[f] * has_before_x
        yield field_at(f, x + 1) if x < CX - 1 else x_after[f] * has_after_x
        at = slice(f * CX + x, f * CX + x + 1)
        yield jnp.where(rows == 0, y_before[at, :] * has_before_y, pltpu.roll(center, 1, 0))
        yield jnp.where(
            rows == CY - 1, y_after[at, :] * has_after_y, pltpu.roll(center, CY - 1, 0)
        )
        part = slice(x * CY, (x + 1) * CY)
        yield jnp.where(lanes == 0, z_low[part, f : f + 1], pltpu.roll(center, 1, 1))
        yield jnp.where(lanes == CZ - 1, z_high[part, f : f + 1], pltpu.roll(center, CZ - 1, 1))

    for x in range(CX):
        visc = viscosity[x]
        weights = [0.5 * (visc + other) for other in neighbours(5, x)]
        for f in range(5):
            center = adjoint[f, x]
            total = jnp.zeros((CY, CZ), F32)
            for weight, other in zip(weights, neighbours(f, x)):
                total = total + weight * (other - center)
            for g in range(5):
                total = total + jacobian[f, g] * adjoint[g, x]
            out[f, x] = center + time_step * total


def solve_kernel(inverse, slots, lift, readout, cell, patch, ranks, partial, updated, shear):
    lift_all = lift[...]
    read = jnp.concatenate([readout[...], jnp.zeros((3, PROF), F32)], axis=0)

    def stack_matrix(matrix):
        high, low = split(matrix)
        return jnp.concatenate(
            [
                jnp.concatenate([high, high], axis=1),
                jnp.concatenate([low, jnp.zeros_like(low)], axis=1),
            ],
            axis=0,
        )

    def product(stacked, right):
        count = stacked.shape[0] // 2
        both = dot(stacked, jnp.concatenate(split(right), axis=0))
        return both[:count] + both[count:]

    read_stack = stack_matrix(read)
    results = []
    for start in range(0, PATCHES, GROUP):
        group = range(start, start + GROUP)
        stacks = [stack_matrix(inverse[p]) for p in group]
        rows = [slots[p] for p in group]
        forcing = [
            jnp.dot(
                lift_all, r[:6], precision=lax.Precision.HIGHEST, preferred_element_type=F32
            )
            for r in rows
        ]
        damping = [0.5 * r[5:6] for r in rows]
        right = forcing
        for sweep in range(ITERS):
            profile = [product(s, r) for s, r in zip(stacks, right)]
            if sweep < ITERS - 1:
                right = [g - d * jnp.tanh(q) for g, d, q in zip(forcing, damping, profile)]
        results += [product(read_stack, q) for q in profile]

    result = jnp.concatenate(results, axis=0)
    rank_hot = one_hot(CAP, ranks[...], BF16)
    back = dot(
        jnp.concatenate(split(result), axis=1), jnp.concatenate([rank_hot, rank_hot], axis=0)
    )
    patches = patch[...]
    wall = jnp.zeros((8, FACES), F32)
    for p in range(PATCHES):
        wall = wall + jnp.where(patches == p, back[p * 8 : (p + 1) * 8], 0.0)
    shear[...] = wall[:5]

    cells = cell[...]
    span_hot = one_hot(CZ, cells & (CZ - 1), BF16)
    row_hot = lax.broadcasted_iota(jnp.int32, (ROWS, FACES), 0) == (cells >> 8)
    high = wall.astype(BF16).astype(F32)
    low = wall - high
    for f in range(5):
        spread = [jnp.where(row_hot, part[f : f + 1], 0.0).astype(BF16) for part in (high, low)]
        source = dot_t(spread[0], span_hot) + dot_t(spread[1], span_hot)
        updated[f] = partial[f] + time_step * source.reshape(CX, CY, CZ)


def shifted(array, axis, step):
    size = lax.axis_size(axis)
    return lax.ppermute(array, axis, [(i, (i + step) % size) for i in range(size)])


def shape(*dims, dtype=F32):
    return jax.ShapeDtypeStruct(dims, dtype)


def body(
    adjoint, viscosity, flux_jacobian, face_cell, face_patch, wall_inverse, lift_matrix, readout
):
    inverses = lax.all_to_all(
        jnp.broadcast_to(wall_inverse, (PATCHES, PROF, PROF)), "gz", 0, 0, tiled=True
    )
    cell = face_cell.reshape(1, FACES)
    patch = face_patch.reshape(1, FACES)
    face_x, face_y, face_z = shape(6, CY, CZ), shape(6 * CX, CZ), shape(8, ROWS)
    x_low, x_high, y_low, y_high, z_low, z_high, slots, ranks = pl.pallas_call(
        gather_kernel,
        out_shape=(
            face_x,
            face_x,
            face_y,
            face_y,
            face_z,
            face_z,
            shape(PATCHES, 8, CAP),
            shape(1, FACES, dtype=jnp.int32),
        ),
        in_specs=[VMEM] * 4,
        out_specs=[VMEM] * 8,
        compiler_params=PARAMS,
        name="gather",
    )(adjoint, viscosity, cell, patch)
    partial = pl.pallas_call(
        stencil_kernel,
        out_shape=shape(5, CX, CY, CZ),
        in_specs=[VMEM, VMEM, SMEM] + [VMEM] * 6,
        out_specs=VMEM,
        compiler_params=PARAMS,
        name="stencil",
    )(
        adjoint,
        viscosity,
        flux_jacobian,
        shifted(x_high, "gx", 1),
        shifted(x_low, "gx", -1),
        shifted(y_high, "gy", 1),
        shifted(y_low, "gy", -1),
        shifted(z_high, "gz", 1),
        shifted(z_low, "gz", -1),
    )
    return pl.pallas_call(
        solve_kernel,
        out_shape=(shape(5, CX, CY, CZ), shape(5, FACES)),
        in_specs=[VMEM] * 8,
        out_specs=[VMEM] * 2,
        compiler_params=PARAMS,
        name="solve",
    )(inverses, slots, lift_matrix, readout, cell, patch, ranks, partial)


def solution(mesh):
    in_specs = (
        P(None, "gx", "gy", "gz"),
        P("gx", "gy", "gz"),
        P(),
        P(("gx", "gy", "gz")),
        P(("gx", "gy", "gz"), None),
        P(("gx", "gy", "gz"), None, None),
        P(),
        P(),
    )
    out_specs = (P(None, "gx", "gy", "gz"), P(None, ("gx", "gy", "gz")))
    return jax.shard_map(body, mesh=mesh, in_specs=in_specs, out_specs=out_specs, check_vma=False)
```

```python
import functools

import jax
import jax.numpy as jnp
from jax import lax
from jax.experimental import pallas as pl
from jax.experimental.pallas import tpu as pltpu
from jax.sharding import PartitionSpec as P

CX = 4
CY = 32
CZ = 256
FACES = 1024
ROWS = CX * CY
PATCHES = 16
HALF = 8
CAP = 128
PROF = 128
ITERS = 6

time_step = 0.08

F32 = jnp.float32
BF16 = jnp.bfloat16
VMEM = pl.BlockSpec(memory_space=pltpu.VMEM)
HBM = pl.BlockSpec(memory_space=pltpu.HBM)
ANY = pl.BlockSpec(memory_space=pl.ANY)
SMEM = pl.BlockSpec(memory_space=pltpu.SMEM)
LONG = pl.CostEstimate(flops=20_000_000_000, bytes_accessed=60_000_000, transcendentals=0)
PARAMS = pltpu.CompilerParams(vmem_limit_bytes=48 * 1024 * 1024)


def split(x):
    high = x.astype(BF16)
    low = (x - high.astype(F32)).astype(BF16)
    return high, low


def dot(a, b):
    return jnp.dot(a, b, preferred_element_type=F32)


def dot_t(a, b):
    return lax.dot_general(a, b, (((1,), (1,)), ((), ())), preferred_element_type=F32)


def one_hot(count, index, dtype):
    numbers = lax.broadcasted_iota(jnp.int32, (count, index.shape[-1]), 0)
    return jnp.where(numbers == index, 1.0, 0.0).astype(dtype)


def parity(axis):
    return lax.axis_index(axis) & 1


def slot_group(patches):
    apart = patches ^ lax.axis_index("gz")
    return ((apart >> 1) & 1) * HALF + (apart & 1) * (HALF // 2) + (apart >> 2)


def load_kernel(
    adjoint_hbm,
    viscosity_hbm,
    cell_hbm,
    patch_hbm,
    inverse_hbm,
    adjoint,
    viscosity,
    cell,
    patch,
    inverse,
    x_one,
    x_two,
    y_one,
    y_two,
    arrivals,
):
    pairs = (
        (viscosity_hbm, viscosity),
        (adjoint_hbm, adjoint),
        (cell_hbm, cell),
        (patch_hbm, patch),
        (inverse_hbm, inverse),
    )
    copies = [
        pltpu.make_async_copy(source, target, arrivals.at[at])
        for at, (source, target) in enumerate(pairs)
    ]
    for copy in copies:
        copy.start()
    odd_x, odd_y = parity("gx"), parity("gy")
    x_first, x_second = (1 - odd_x) * (CX - 1), odd_x * (CX - 1)
    copies[0].wait()
    copies[1].wait()
    for f in range(6):
        field = viscosity if f == 5 else adjoint.at[f]
        x_one[f] = field[x_first]
        x_two[f] = field[x_second]
        for x in range(CX):
            low, high = field[x, 0:1, :], field[x, CY - 1 : CY, :]
            at = slice(f * CX + x, f * CX + x + 1)
            y_one[at, :] = jnp.where(odd_y == 1, low, high)
            y_two[at, :] = jnp.where(odd_y == 1, high, low)
    for copy in copies[2:]:
        copy.wait()


def gather_kernel(
    adjoint, viscosity, cell, patch, z_one, z_two, own, other, ranks
):
    odd_z = parity("gz")
    cells = cell[...]
    patches = slot_group(patch[...])
    row = cells >> 8
    span = cells & (CZ - 1)
    span_hot = one_hot(CZ, span, BF16)
    row_hot = lax.broadcasted_iota(jnp.int32, (ROWS, FACES), 0) == row
    columns = lax.broadcasted_iota(jnp.int32, (ROWS, 128), 1)
    z_low = z_high = jnp.zeros((ROWS, 128), F32)
    values = []
    for f in range(6):
        field = (viscosity[...] if f == 5 else adjoint[f]).reshape(ROWS, CZ)
        both = dot(jnp.concatenate(split(field), axis=0), span_hot)
        found = both[:ROWS] + both[ROWS:]
        values.append(jnp.sum(jnp.where(row_hot, found, 0.0), axis=0, keepdims=True))
        z_low = jnp.where(columns == f, field[:, 0:1], z_low)
        z_high = jnp.where(columns == f, field[:, CZ - 1 : CZ], z_high)
    z_low, z_high = jnp.transpose(z_low)[:8], jnp.transpose(z_high)[:8]
    z_one[...] = jnp.where(odd_z == 1, z_low, z_high)
    z_two[...] = jnp.where(odd_z == 1, z_high, z_low)

    hot = one_hot(PATCHES, patches, F32)
    pieces = FACES // 128
    stacked = jnp.concatenate([hot[:, b * 128 : (b + 1) * 128] for b in range(pieces)], axis=0)
    stacked = stacked.astype(BF16)
    upto = (
        lax.broadcasted_iota(jnp.int32, (128, 256), 0)
        <= lax.broadcasted_iota(jnp.int32, (128, 256), 1)
    )
    counts = dot(stacked, jnp.where(upto, 1.0, 0.0).astype(BF16))
    earlier = jnp.zeros((PATCHES, 128), F32)
    found_ranks = []
    for b in range(pieces):
        mine = slice(b * PATCHES, (b + 1) * PATCHES)
        piece = hot[:, b * 128 : (b + 1) * 128]
        found_ranks.append(
            jnp.sum(piece * (counts[mine, :128] + earlier), axis=0, keepdims=True) - 1.0
        )
        earlier = earlier + counts[mine, 128:]
    rank = jnp.concatenate(found_ranks, axis=1).astype(jnp.int32)
    ranks[...] = rank

    rank_hot = one_hot(CAP, rank, BF16)
    table = jnp.concatenate(values + [jnp.zeros((2, FACES), F32)], axis=0)
    high, low = split(table)
    both = jnp.concatenate([high.astype(F32), low.astype(F32)], axis=0)
    spread = jnp.concatenate(
        [jnp.where(patches == p, both, 0.0).astype(BF16) for p in range(PATCHES)], axis=0
    )
    placed = dot_t(spread, rank_hot).reshape(PATCHES, 16, CAP)
    slots = placed[:, :8] + placed[:, 8:]
    own[...] = slots[:HALF]
    other[...] = slots[HALF:]


def stencil_kernel(
    adjoint, viscosity, jacobian, x_one, x_two, y_one, y_two, z_one, after, out
):
    def sides(axis, one, two):
        odd = parity(axis) == 1
        return jnp.where(odd, one, two), jnp.where(odd, two, one)

    gx, gy = lax.axis_index("gx"), lax.axis_index("gy")
    has_before_x = jnp.where(gx > 0, 1.0, 0.0)
    has_after_x = jnp.where(gx < lax.axis_size("gx") - 1, 1.0, 0.0)
    has_before_y = jnp.where(gy > 0, 1.0, 0.0)
    has_after_y = jnp.where(gy < lax.axis_size("gy") - 1, 1.0, 0.0)
    y_before, y_after = sides("gy", y_one[...], y_two[...])
    y_before, y_after = y_before * has_before_y, y_after * has_after_y
    z_side = jnp.transpose(z_one[4 * PROF :, :])
    odd_z = parity("gz")

    def x_side(f, side):
        before, after = sides("gx", x_one[f], x_two[f])
        return after * has_after_x if side else before * has_before_x

    rows = lax.broadcasted_iota(jnp.int32, (CY, CZ), 0)
    lanes = lax.broadcasted_iota(jnp.int32, (CY, CZ), 1)
    def field_at(f, x):
        return viscosity[x] if f == 5 else adjoint[f, x]

    def neighbours(f, x):
        center = field_at(f, x)
        yield field_at(f, x - 1) if x > 0 else x_side(f, 0)
        yield field_at(f, x + 1) if x < CX - 1 else x_side(f, 1)
        at = slice(f * CX + x, f * CX + x + 1)
        yield jnp.where(rows == 0, y_before[at, :], pltpu.roll(center, 1, 0))
        yield jnp.where(
            rows == CY - 1, y_after[at, :], pltpu.roll(center, CY - 1, 0)
        )
        part = slice(x * CY, (x + 1) * CY)
        low, high = pltpu.roll(center, 1, 1), pltpu.roll(center, CZ - 1, 1)
        edge = z_side[part, f : f + 1]
        low = jnp.where((lanes == 0) & (odd_z == 1), edge, low)
        high = jnp.where((lanes == CZ - 1) & (odd_z == 0), edge, high)
        yield jnp.where((lanes == 0) & (odd_z == 0), center, low)
        yield jnp.where((lanes == CZ - 1) & (odd_z == 1), center, high)

    for x in range(CX):
        visc = viscosity[x]
        weights = [0.5 * (visc + other) for other in neighbours(5, x)]
        for f in range(5):
            center = adjoint[f, x]
            total = jnp.zeros((CY, CZ), F32)
            for weight, other in zip(weights, neighbours(f, x)):
                total = total + weight * (other - center)
            for g in range(5):
                total = total + jacobian[f, g] * adjoint[g, x]
            out[f, x] = center + time_step * total


def wide(matrix):
    high, low = split(matrix)
    return jnp.concatenate([high, low, high], axis=1)


def product(left, right):
    high, low = split(right)
    return dot(left, jnp.concatenate([high, high, low], axis=0))


def join_kernel(first, second, third, fourth, edge, before, joined):
    for at, block in enumerate((first, second, third, fourth)):
        joined[at * PROF : (at + 1) * PROF, :] = block[0]
    joined[4 * PROF :, :] = edge[...]


def solve_kernel(mine, theirs, own, arrived, lift, readout, solved_own, solved_arrived):
    inverse = [
        ref[at * PROF : (at + 1) * PROF, :] for ref in (mine, theirs) for at in range(HALF // 2)
    ]
    read = wide(jnp.concatenate([readout[...], jnp.zeros((3, PROF), F32)], axis=0))
    spread = wide(lift[...])
    inverses = [wide(inverse[p]) for p in range(HALF)]
    folded = [wide(product(read, inverse[p])) for p in range(HALF)]
    rows = [jnp.concatenate([own[p], arrived[p]], axis=1) for p in range(HALF)]
    forcing = [product(spread, r[:6]) for r in rows]
    damping = [0.5 * r[5:6] for r in rows]
    right = forcing
    for sweep in range(ITERS - 1):
        profile = [product(w, r) for w, r in zip(inverses, right)]
        right = [g - d * jnp.tanh(q) for g, d, q in zip(forcing, damping, profile)]
    for p in range(HALF):
        result = product(folded[p], right[p])
        solved_own[p] = result[:, :CAP]
        solved_arrived[p] = result[:, CAP:]


def scatter_kernel(
    solved_own,
    returned,
    cell,
    patch,
    ranks,
    partial,
    adjoint,
    viscosity,
    z_two,
    updated,
    shear,
):
    result = jnp.concatenate([solved_own[...], returned[...]], axis=0).reshape(PATCHES * 8, CAP)
    rank_hot = one_hot(CAP, ranks[...], BF16)
    back = dot(
        jnp.concatenate(split(result), axis=1), jnp.concatenate([rank_hot, rank_hot], axis=0)
    )
    patches = slot_group(patch[...])
    wall = jnp.zeros((8, FACES), F32)
    for p in range(PATCHES):
        wall = wall + jnp.where(patches == p, back[p * 8 : (p + 1) * 8], 0.0)
    shear[...] = wall[:5]

    side = jnp.transpose(z_two[...])
    lane = parity("gz") * (CZ - 1)
    lanes = lax.broadcasted_iota(jnp.int32, (ROWS, CZ), 1)
    visc = viscosity[...].reshape(ROWS, CZ)
    at_edge = jnp.where(lanes == lane, 0.5 * (visc + side[:, 5:6]), 0.0)
    cells = cell[...]
    span_hot = one_hot(CZ, cells & (CZ - 1), BF16)
    row_hot = lax.broadcasted_iota(jnp.int32, (ROWS, FACES), 0) == (cells >> 8)
    high = wall.astype(BF16).astype(F32)
    low = wall - high
    for f in range(5):
        spread = [jnp.where(row_hot, part[f : f + 1], 0.0).astype(BF16) for part in (high, low)]
        both = dot_t(jnp.concatenate(spread, axis=0), span_hot)
        source = both[:ROWS] + both[ROWS:]
        value = adjoint[f].reshape(ROWS, CZ)
        edge = at_edge * (side[:, f : f + 1] - value)
        updated[f] = partial[f] + (time_step * (source + edge)).reshape(CX, CY, CZ)


def swapped(array, axis, partner):
    return lax.ppermute(array, axis, [(i, partner(i)) for i in range(lax.axis_size(axis))])


def first_side(array, axis):
    return swapped(array, axis, lambda i: i ^ 1)


def second_side(array, axis):
    size = lax.axis_size(axis)
    return swapped(array, axis, lambda i: (i + 1 if i % 2 else i - 1) % size)


def shape(*dims, dtype=F32):
    return jax.ShapeDtypeStruct(dims, dtype)


def body(
    adjoint, viscosity, flux_jacobian, face_cell, face_patch, wall_inverse, lift_matrix, readout
):
    cell = face_cell.reshape(1, FACES)
    patch = face_patch.reshape(1, FACES)
    face_x, face_y, face_z = shape(6, CY, CZ), shape(6 * CX, CZ), shape(8, ROWS)
    slots, numbers = shape(HALF, 8, CAP), shape(1, FACES, dtype=jnp.int32)
    arrays = [adjoint, viscosity, cell, patch, wall_inverse]
    adjoint, viscosity, cell, patch, inverse, x_one, x_two, y_one, y_two = pl.pallas_call(
        load_kernel,
        out_shape=tuple(shape(*a.shape, dtype=a.dtype) for a in arrays)
        + (face_x, face_x, face_y, face_y),
        in_specs=[HBM] * 5,
        out_specs=[VMEM] * 9,
        scratch_shapes=[pltpu.SemaphoreType.DMA((5,))],
        compiler_params=PARAMS,
        name="load",
    )(*[pltpu.with_memory_space_constraint(a, pltpu.HBM) for a in arrays])
    blocks = [inverse]
    for step in range(1, 4):
        blocks.append(swapped(inverse, "gz", lambda i: i ^ (4 * step)))
    y_two = second_side(y_two, "gy")
    z_one, z_two, own, other, ranks = pl.pallas_call(
        gather_kernel,
        out_shape=(face_z, face_z, slots, slots, numbers),
        in_specs=[VMEM] * 4,
        out_specs=[VMEM] * 5,
        compiler_params=PARAMS,
        name="gather",
    )(adjoint, viscosity, cell, patch)
    arrived = swapped(other, "gz", lambda i: i ^ 2)
    mine = pl.pallas_call(
        join_kernel,
        out_shape=shape(4 * PROF + 8, PROF),
        in_specs=[VMEM] * 5 + [ANY],
        out_specs=VMEM,
        compiler_params=PARAMS,
        name="join",
    )(*blocks, z_one, y_two)
    theirs = swapped(mine, "gz", lambda i: i ^ 1)
    solved_own, solved_arrived = pl.pallas_call(
        solve_kernel,
        out_shape=(slots, slots),
        in_specs=[VMEM] * 6,
        out_specs=[VMEM] * 2,
        compiler_params=PARAMS,
        cost_estimate=LONG,
        name="solve",
    )(mine, theirs, own, arrived, lift_matrix, readout)
    returned = swapped(solved_arrived, "gz", lambda i: i ^ 2)
    partial = pl.pallas_call(
        stencil_kernel,
        out_shape=shape(5, CX, CY, CZ),
        in_specs=[VMEM, VMEM, SMEM] + [VMEM] * 5 + [ANY],
        out_specs=VMEM,
        compiler_params=PARAMS,
        cost_estimate=LONG,
        name="stencil",
    )(
        adjoint,
        viscosity,
        flux_jacobian,
        first_side(x_one, "gx"),
        second_side(x_two, "gx"),
        first_side(y_one, "gy"),
        y_two,
        theirs,
        solved_own,
    )
    return pl.pallas_call(
        scatter_kernel,
        out_shape=(shape(5, CX, CY, CZ), shape(5, FACES)),
        in_specs=[VMEM] * 9,
        out_specs=[VMEM] * 2,
        compiler_params=PARAMS,
        name="scatter",
    )(
        solved_own,
        returned,
        cell,
        patch,
        ranks,
        partial,
        adjoint,
        viscosity,
        second_side(z_two, "gz"),
    )


def solution(mesh):
    in_specs = (
        P(None, "gx", "gy", "gz"),
        P("gx", "gy", "gz"),
        P(),
        P(("gx", "gy", "gz")),
        P(("gx", "gy", "gz"), None),
        P(("gx", "gy", "gz"), None, None),
        P(),
        P(),
    )
    out_specs = (P(None, "gx", "gy", "gz"), P(None, ("gx", "gy", "gz")))
    return jax.shard_map(body, mesh=mesh, in_specs=in_specs, out_specs=out_specs, check_vma=False)
```

```python
import functools

import jax
import jax.numpy as jnp
from jax import lax
from jax.experimental import pallas as pl
from jax.experimental.pallas import tpu as pltpu
from jax.sharding import PartitionSpec as P

CX = 4
CY = 32
CZ = 256
FACES = 1024
ROWS = CX * CY
PATCHES = 16
HALF = 8
CAP = 128
PROF = 128
ITERS = 6

time_step = 0.08

F32 = jnp.float32
BF16 = jnp.bfloat16
VMEM = pl.BlockSpec(memory_space=pltpu.VMEM)
HBM = pl.BlockSpec(memory_space=pltpu.HBM)
ANY = pl.BlockSpec(memory_space=pl.ANY)
SMEM = pl.BlockSpec(memory_space=pltpu.SMEM)
LONG = pl.CostEstimate(flops=20_000_000_000, bytes_accessed=60_000_000, transcendentals=0)
PARAMS = pltpu.CompilerParams(vmem_limit_bytes=48 * 1024 * 1024)


def split(x):
    high = x.astype(BF16)
    low = (x - high.astype(F32)).astype(BF16)
    return high, low


def dot(a, b):
    return jnp.dot(a, b, preferred_element_type=F32)


def dot_t(a, b):
    return lax.dot_general(a, b, (((1,), (1,)), ((), ())), preferred_element_type=F32)


def one_hot(count, index, dtype):
    numbers = lax.broadcasted_iota(jnp.int32, (count, index.shape[-1]), 0)
    return jnp.where(numbers == index, 1.0, 0.0).astype(dtype)


def parity(axis):
    return lax.axis_index(axis) & 1


def slot_group(patches):
    apart = patches ^ lax.axis_index("gz")
    return ((apart >> 1) & 1) * HALF + (apart & 1) * (HALF // 2) + (apart >> 2)


def load_kernel(
    adjoint_hbm,
    viscosity_hbm,
    cell_hbm,
    patch_hbm,
    inverse_hbm,
    adjoint,
    viscosity,
    cell,
    patch,
    package,
    y_one,
    z_one,
    arrivals,
):
    pairs = (
        (viscosity_hbm, viscosity),
        (adjoint_hbm, adjoint),
        (cell_hbm, cell),
        (patch_hbm, patch),
        (inverse_hbm, package.at[:, :PROF]),
    )
    copies = [
        pltpu.make_async_copy(source, target, arrivals.at[at])
        for at, (source, target) in enumerate(pairs)
    ]
    for copy in copies:
        copy.start()
    copies[0].wait()
    copies[1].wait()
    odd_y = parity("gy")
    for f in range(6):
        field = viscosity if f == 5 else adjoint.at[f]
        for x in range(CX):
            low, high = field[x, 0:1, :], field[x, CY - 1 : CY, :]
            at = slice(f * CX + x, f * CX + x + 1)
            y_one[at, :] = jnp.where(odd_y == 1, low, high)
    columns = lax.broadcasted_iota(jnp.int32, (ROWS, 128), 1)
    z_low = z_high = jnp.zeros((ROWS, 128), F32)
    for f in range(6):
        field = (viscosity[...] if f == 5 else adjoint[f]).reshape(ROWS, CZ)
        z_low = jnp.where(columns == f, field[:, 0:1], z_low)
        z_high = jnp.where(columns == f, field[:, CZ - 1 : CZ], z_high)
    z_low, z_high = jnp.transpose(z_low)[:8], jnp.transpose(z_high)[:8]
    odd_z = parity("gz") == 1
    z_one[...] = jnp.where(odd_z, z_low, z_high)
    package[0, PROF:, :] = jnp.where(odd_z, z_high, z_low)
    for copy in copies[2:]:
        copy.wait()


def early_kernel(
    adjoint, viscosity, cell, patch, before, joined, y_two, own, other, ranks
):
    odd_y = parity("gy")
    for f in range(6):
        field = viscosity if f == 5 else adjoint.at[f]
        for x in range(CX):
            low, high = field[x, 0:1, :], field[x, CY - 1 : CY, :]
            at = slice(f * CX + x, f * CX + x + 1)
            y_two[at, :] = jnp.where(odd_y == 1, high, low)
    results = (own, other, ranks)
    near = lax.axis_index("gy") < lax.axis_size("gy") // 2

    @pl.when(near)
    def _():
        gather(adjoint, viscosity, cell, patch, *results)

    @pl.when(jnp.logical_not(near))
    def _():
        for ref in results:
            ref[...] = jnp.zeros(ref.shape, ref.dtype)


def late_kernel(adjoint, viscosity, cell, patch, *refs):
    near = lax.axis_index("gy") < lax.axis_size("gy") // 2

    @pl.when(near)
    def _():
        for found, result in zip(refs[:3], refs[3:]):
            result[...] = found[...]

    @pl.when(jnp.logical_not(near))
    def _():
        gather(adjoint, viscosity, cell, patch, *refs[3:])


def faces_kernel(adjoint, viscosity, rows, before, x_one, x_two, sent):
    sent[...] = rows[...]
    odd_x = parity("gx")
    x_first, x_second = (1 - odd_x) * (CX - 1), odd_x * (CX - 1)
    for f in range(6):
        field = viscosity if f == 5 else adjoint.at[f]
        x_one[f] = field[x_first]
        x_two[f] = field[x_second]


def gather(adjoint, viscosity, cell, patch, own, other, ranks):
    cells = cell[...]
    patches = slot_group(patch[...])
    row = cells >> 8
    span = cells & (CZ - 1)
    span_hot = one_hot(CZ, span, BF16)
    row_hot = lax.broadcasted_iota(jnp.int32, (ROWS, FACES), 0) == row
    values = []
    for f in range(6):
        field = (viscosity[...] if f == 5 else adjoint[f]).reshape(ROWS, CZ)
        both = dot(jnp.concatenate(split(field), axis=0), span_hot)
        found = both[:ROWS] + both[ROWS:]
        values.append(jnp.sum(jnp.where(row_hot, found, 0.0), axis=0, keepdims=True))

    hot = one_hot(PATCHES, patches, F32)
    pieces = FACES // 128
    stacked = jnp.concatenate([hot[:, b * 128 : (b + 1) * 128] for b in range(pieces)], axis=0)
    stacked = stacked.astype(BF16)
    upto = (
        lax.broadcasted_iota(jnp.int32, (128, 256), 0)
        <= lax.broadcasted_iota(jnp.int32, (128, 256), 1)
    )
    counts = dot(stacked, jnp.where(upto, 1.0, 0.0).astype(BF16))
    earlier = jnp.zeros((PATCHES, 128), F32)
    found_ranks = []
    for b in range(pieces):
        mine = slice(b * PATCHES, (b + 1) * PATCHES)
        piece = hot[:, b * 128 : (b + 1) * 128]
        found_ranks.append(
            jnp.sum(piece * (counts[mine, :128] + earlier), axis=0, keepdims=True) - 1.0
        )
        earlier = earlier + counts[mine, 128:]
    rank = jnp.concatenate(found_ranks, axis=1).astype(jnp.int32)
    ranks[...] = rank

    rank_hot = one_hot(CAP, rank, BF16)
    table = jnp.concatenate(values + [jnp.zeros((2, FACES), F32)], axis=0)
    high, low = split(table)
    both = jnp.concatenate([high.astype(F32), low.astype(F32)], axis=0)
    spread = jnp.concatenate(
        [jnp.where(patches == p, both, 0.0).astype(BF16) for p in range(PATCHES)], axis=0
    )
    placed = dot_t(spread, rank_hot).reshape(PATCHES, 16, CAP)
    slots = placed[:, :8] + placed[:, 8:]
    for p in range(HALF):
        own[p * 6 : (p + 1) * 6, :] = slots[p, :6]
        other[p * 6 : (p + 1) * 6, :] = slots[HALF + p, :6]


def stencil_kernel(
    adjoint, viscosity, jacobian, x_one, x_two, y_one, y_two, z_one, after, out
):
    def sides(axis, one, two):
        odd = parity(axis) == 1
        return jnp.where(odd, one, two), jnp.where(odd, two, one)

    gx, gy = lax.axis_index("gx"), lax.axis_index("gy")
    has_before_x = jnp.where(gx > 0, 1.0, 0.0)
    has_after_x = jnp.where(gx < lax.axis_size("gx") - 1, 1.0, 0.0)
    has_before_y = jnp.where(gy > 0, 1.0, 0.0)
    has_after_y = jnp.where(gy < lax.axis_size("gy") - 1, 1.0, 0.0)
    y_before, y_after = sides("gy", y_one[...], y_two[...])
    y_before, y_after = y_before * has_before_y, y_after * has_after_y
    z_side = jnp.transpose(z_one[4 * PROF : 4 * PROF + 8, :])
    odd_z = parity("gz")

    def x_side(f, side):
        before, after = sides("gx", x_one[f], x_two[f])
        return after * has_after_x if side else before * has_before_x

    rows = lax.broadcasted_iota(jnp.int32, (CY, CZ), 0)
    lanes = lax.broadcasted_iota(jnp.int32, (CY, CZ), 1)
    def field_at(f, x):
        return viscosity[x] if f == 5 else adjoint[f, x]

    def neighbours(f, x):
        center = field_at(f, x)
        yield field_at(f, x - 1) if x > 0 else x_side(f, 0)
        yield field_at(f, x + 1) if x < CX - 1 else x_side(f, 1)
        at = slice(f * CX + x, f * CX + x + 1)
        yield jnp.where(rows == 0, y_before[at, :], pltpu.roll(center, 1, 0))
        yield jnp.where(
            rows == CY - 1, y_after[at, :], pltpu.roll(center, CY - 1, 0)
        )
        part = slice(x * CY, (x + 1) * CY)
        low, high = pltpu.roll(center, 1, 1), pltpu.roll(center, CZ - 1, 1)
        edge = z_side[part, f : f + 1]
        low = jnp.where((lanes == 0) & (odd_z == 1), edge, low)
        high = jnp.where((lanes == CZ - 1) & (odd_z == 0), edge, high)
        yield jnp.where((lanes == 0) & (odd_z == 0), center, low)
        yield jnp.where((lanes == CZ - 1) & (odd_z == 1), center, high)

    for x in range(CX):
        visc = viscosity[x]
        weights = [0.5 * (visc + other) for other in neighbours(5, x)]
        for f in range(5):
            center = adjoint[f, x]
            total = jnp.zeros((CY, CZ), F32)
            for weight, other in zip(weights, neighbours(f, x)):
                total = total + weight * (other - center)
            for g in range(5):
                total = total + jacobian[f, g] * adjoint[g, x]
            out[f, x] = center + time_step * total


def wide(matrix):
    high, low = split(matrix)
    return jnp.concatenate([high, low, high], axis=1)


def product(left, right):
    high, low = split(right)
    return dot(left, jnp.concatenate([high, high, low], axis=0))


def join_kernel(first, second, third, fourth, edge, joined):
    for at, block in enumerate((first, second, third, fourth)):
        joined[at * PROF : (at + 1) * PROF, :] = block[0, :PROF, :]
    place = lax.axis_index("gz")
    inner = (place ^ (place >> 1)) & 1 == 1
    nearer = (place >> 2) & 1 == (place >> 1) & 1
    passed = jnp.where(nearer, second[0, PROF:, :], fourth[0, PROF:, :])
    joined[4 * PROF : 4 * PROF + 8, :] = edge[...]
    joined[4 * PROF + 8 :, :] = jnp.where(inner, first[0, PROF:, :], passed)


def solve_kernel(mine, theirs, rows, lift, readout, *refs):
    solved = refs[-1]
    inverse = [
        ref[at * PROF : (at + 1) * PROF, :] for ref in (mine, theirs) for at in range(HALF // 2)
    ]
    read = wide(jnp.concatenate([readout[...], jnp.zeros((3, PROF), F32)], axis=0))
    spread = wide(lift[...])
    inverses = [wide(inverse[p]) for p in range(HALF)]
    folded = [wide(product(read, inverse[p])) for p in range(HALF)]
    rows = [rows[p * 6 : (p + 1) * 6, :] for p in range(HALF)]
    forcing = [product(spread, r) for r in rows]
    damping = [0.5 * r[5:6] for r in rows]
    right = forcing
    for sweep in range(ITERS - 1):
        profile = [product(w, r) for w, r in zip(inverses, right)]
        right = [g - d * jnp.tanh(q) for g, d, q in zip(forcing, damping, profile)]
    for p in range(HALF):
        result = product(folded[p], right[p])
        for f in range(5):
            solved[f * HALF + p : f * HALF + p + 1, :] = result[f : f + 1]
    solved[5 * HALF :, :] = theirs[4 * PROF + 8 :, :]


def scatter_kernel(
    solved_own,
    returned,
    cell,
    patch,
    ranks,
    partial,
    adjoint,
    viscosity,
    updated,
    shear,
):
    parts = (solved_own[: 5 * HALF, :], returned[: 5 * HALF, :])
    result = jnp.concatenate(parts, axis=0)
    rank_hot = one_hot(CAP, ranks[...], BF16)
    back = dot(
        jnp.concatenate(split(result), axis=1), jnp.concatenate([rank_hot, rank_hot], axis=0)
    )
    patches = slot_group(patch[...])
    numbers = lax.broadcasted_iota(jnp.int32, (HALF, FACES), 0)
    kept = [numbers == patches, numbers + HALF == patches]
    walls = []
    for f in range(5):
        parts = [back[at + f * HALF : at + (f + 1) * HALF] for at in (0, 5 * HALF)]
        both = jnp.where(kept[0], parts[0], 0.0) + jnp.where(kept[1], parts[1], 0.0)
        walls.append(jnp.sum(both, axis=0, keepdims=True))
    wall = jnp.concatenate(walls + [jnp.zeros((3, FACES), F32)], axis=0)
    shear[...] = wall[:5]

    side = jnp.transpose(returned[5 * HALF :, :])
    lane = parity("gz") * (CZ - 1)
    lanes = lax.broadcasted_iota(jnp.int32, (ROWS, CZ), 1)
    visc = viscosity[...].reshape(ROWS, CZ)
    at_edge = jnp.where(lanes == lane, 0.5 * (visc + side[:, 5:6]), 0.0)
    cells = cell[...]
    span_hot = one_hot(CZ, cells & (CZ - 1), BF16)
    row_hot = lax.broadcasted_iota(jnp.int32, (ROWS, FACES), 0) == (cells >> 8)
    high = wall.astype(BF16).astype(F32)
    low = wall - high
    for f in range(5):
        spread = [jnp.where(row_hot, part[f : f + 1], 0.0).astype(BF16) for part in (high, low)]
        both = dot_t(jnp.concatenate(spread, axis=0), span_hot)
        source = both[:ROWS] + both[ROWS:]
        value = adjoint[f].reshape(ROWS, CZ)
        edge = at_edge * (side[:, f : f + 1] - value)
        updated[f] = partial[f] + (time_step * (source + edge)).reshape(CX, CY, CZ)


def swapped(array, axis, partner):
    return lax.ppermute(array, axis, [(i, partner(i)) for i in range(lax.axis_size(axis))])


def first_side(array, axis):
    return swapped(array, axis, lambda i: i ^ 1)


def second_side(array, axis):
    size = lax.axis_size(axis)
    return swapped(array, axis, lambda i: (i + 1 if i % 2 else i - 1) % size)


def shape(*dims, dtype=F32):
    return jax.ShapeDtypeStruct(dims, dtype)


def body(
    adjoint, viscosity, flux_jacobian, face_cell, face_patch, wall_inverse, lift_matrix, readout
):
    cell = face_cell.reshape(1, FACES)
    patch = face_patch.reshape(1, FACES)
    face_x, face_y, face_z = shape(6, CY, CZ), shape(6 * CX, CZ), shape(8, ROWS)
    slots, numbers = shape(HALF * 6, CAP), shape(1, FACES, dtype=jnp.int32)
    arrays = [adjoint, viscosity, cell, patch, wall_inverse]
    package = shape(1, PROF + 8, PROF)
    adjoint, viscosity, cell, patch, package, y_one, z_one = pl.pallas_call(
        load_kernel,
        out_shape=tuple(shape(*a.shape, dtype=a.dtype) for a in arrays[:4])
        + (package, face_y, face_z),
        in_specs=[HBM] * 5,
        out_specs=[VMEM] * 7,
        scratch_shapes=[pltpu.SemaphoreType.DMA((5,))],
        compiler_params=PARAMS,
        name="load",
    )(*[pltpu.with_memory_space_constraint(a, pltpu.HBM) for a in arrays])
    blocks = [package]
    for step in range(1, 4):
        blocks.append(swapped(package, "gz", lambda i: i ^ (4 * step)))
    mine = pl.pallas_call(
        join_kernel,
        out_shape=shape(4 * PROF + 16, PROF),
        in_specs=[VMEM] * 5,
        out_specs=VMEM,
        compiler_params=PARAMS,
        name="join",
    )(*blocks, z_one)
    theirs = swapped(mine, "gz", lambda i: i ^ 1)
    fields = (adjoint, viscosity, cell, patch)
    gathered = (slots, slots, numbers)
    y_one = first_side(y_one, "gy")
    y_two, *found = pl.pallas_call(
        early_kernel,
        out_shape=(face_y,) + gathered,
        in_specs=[VMEM] * 4 + [ANY] * 2,
        out_specs=[VMEM] * 4,
        compiler_params=PARAMS,
        name="early_gather",
    )(*fields, y_one, y_one)
    y_two = second_side(y_two, "gy")
    own, other, ranks = pl.pallas_call(
        late_kernel,
        out_shape=gathered,
        in_specs=[VMEM] * 7,
        out_specs=[VMEM] * 3,
        compiler_params=PARAMS,
        cost_estimate=LONG,
        name="late_gather",
    )(*fields, *found)
    x_one, x_two, other = pl.pallas_call(
        faces_kernel,
        out_shape=(face_x, face_x, slots),
        in_specs=[VMEM, VMEM, VMEM, ANY],
        out_specs=[VMEM] * 3,
        compiler_params=PARAMS,
        cost_estimate=LONG,
        name="faces",
    )(adjoint, viscosity, other, y_two)
    arrived = swapped(other, "gz", lambda i: i ^ 2)
    def solve(rows, *after):
        return pl.pallas_call(
            solve_kernel,
            out_shape=shape(5 * HALF + 8, CAP),
            in_specs=[VMEM] * 5 + [ANY] * len(after),
            out_specs=VMEM,
            compiler_params=PARAMS,
            cost_estimate=LONG,
            name="solve",
        )(mine, theirs, rows, lift_matrix, readout, *after)

    solved_arrived = solve(arrived)
    returned = swapped(solved_arrived, "gz", lambda i: i ^ 2)
    solved_own = solve(own, solved_arrived)
    partial = pl.pallas_call(
        stencil_kernel,
        out_shape=shape(5, CX, CY, CZ),
        in_specs=[VMEM, VMEM, SMEM] + [VMEM] * 5 + [ANY],
        out_specs=VMEM,
        compiler_params=PARAMS,
        cost_estimate=LONG,
        name="stencil",
    )(
        adjoint,
        viscosity,
        flux_jacobian,
        first_side(x_one, "gx"),
        second_side(x_two, "gx"),
        y_one,
        y_two,
        theirs,
        solved_own,
    )
    return pl.pallas_call(
        scatter_kernel,
        out_shape=(shape(5, CX, CY, CZ), shape(5, FACES)),
        in_specs=[VMEM] * 8,
        out_specs=[VMEM] * 2,
        compiler_params=PARAMS,
        name="scatter",
    )(
        solved_own,
        returned,
        cell,
        patch,
        ranks,
        partial,
        adjoint,
        viscosity,
    )


def solution(mesh):
    in_specs = (
        P(None, "gx", "gy", "gz"),
        P("gx", "gy", "gz"),
        P(),
        P(("gx", "gy", "gz")),
        P(("gx", "gy", "gz"), None),
        P(("gx", "gy", "gz"), None, None),
        P(),
        P(),
    )
    out_specs = (P(None, "gx", "gy", "gz"), P(None, ("gx", "gy", "gz")))
    return jax.shard_map(body, mesh=mesh, in_specs=in_specs, out_specs=out_specs, check_vma=False)
```

```python
import functools

import jax
import jax.numpy as jnp
from jax import lax
from jax.experimental import pallas as pl
from jax.experimental.pallas import tpu as pltpu
from jax.sharding import PartitionSpec as P

CX = 4
CY = 32
CZ = 256
FACES = 1024
ROWS = CX * CY
PATCHES = 16
HALF = 8
CAP = 128
PROF = 128
ITERS = 6

time_step = 0.08

F32 = jnp.float32
BF16 = jnp.bfloat16
VMEM = pl.BlockSpec(memory_space=pltpu.VMEM)
HBM = pl.BlockSpec(memory_space=pltpu.HBM)
ANY = pl.BlockSpec(memory_space=pl.ANY)
SMEM = pl.BlockSpec(memory_space=pltpu.SMEM)
LONG = pl.CostEstimate(flops=20_000_000_000, bytes_accessed=60_000_000, transcendentals=0)
SHORT = pl.CostEstimate(flops=1000, bytes_accessed=1000, transcendentals=0)
PARAMS = pltpu.CompilerParams(vmem_limit_bytes=48 * 1024 * 1024)


def split(x):
    high = x.astype(BF16)
    low = (x - high.astype(F32)).astype(BF16)
    return high, low


def dot(a, b):
    return jnp.dot(a, b, preferred_element_type=F32)


def dot_t(a, b):
    return lax.dot_general(a, b, (((1,), (1,)), ((), ())), preferred_element_type=F32)


def one_hot(count, index, dtype):
    numbers = lax.broadcasted_iota(jnp.int32, (count, index.shape[-1]), 0)
    return jnp.where(numbers == index, 1.0, 0.0).astype(dtype)


def parity(axis):
    return lax.axis_index(axis) & 1


def slot_group(patches):
    apart = patches ^ lax.axis_index("gz")
    return ((apart >> 1) & 1) * HALF + (apart & 1) * (HALF // 2) + (apart >> 2)


def load_kernel(
    adjoint_hbm,
    viscosity_hbm,
    cell_hbm,
    patch_hbm,
    inverse_hbm,
    adjoint,
    viscosity,
    cell,
    patch,
    package,
    y_one,
    z_one,
    arrivals,
):
    pairs = (
        (viscosity_hbm, viscosity),
        (adjoint_hbm, adjoint),
        (cell_hbm, cell),
        (patch_hbm, patch),
        (inverse_hbm, package.at[:, :PROF]),
    )
    copies = [
        pltpu.make_async_copy(source, target, arrivals.at[at])
        for at, (source, target) in enumerate(pairs)
    ]
    for copy in copies:
        copy.start()
    copies[0].wait()
    copies[1].wait()
    odd_y = parity("gy")
    for f in range(6):
        field = viscosity if f == 5 else adjoint.at[f]
        for x in range(CX):
            low, high = field[x, 0:1, :], field[x, CY - 1 : CY, :]
            at = slice(f * CX + x, f * CX + x + 1)
            y_one[at, :] = jnp.where(odd_y == 1, low, high)
    columns = lax.broadcasted_iota(jnp.int32, (ROWS, 128), 1)
    z_low = z_high = jnp.zeros((ROWS, 128), F32)
    for f in range(6):
        field = (viscosity[...] if f == 5 else adjoint[f]).reshape(ROWS, CZ)
        z_low = jnp.where(columns == f, field[:, 0:1], z_low)
        z_high = jnp.where(columns == f, field[:, CZ - 1 : CZ], z_high)
    z_low, z_high = jnp.transpose(z_low)[:8], jnp.transpose(z_high)[:8]
    odd_z = parity("gz") == 1
    z_one[...] = jnp.where(odd_z, z_low, z_high)
    package[0, PROF:, :] = jnp.where(odd_z, z_high, z_low)
    for copy in copies[2:]:
        copy.wait()


def early_kernel(
    adjoint, viscosity, cell, patch, before, joined, y_two, own, other, ranks
):
    odd_y = parity("gy")
    for f in range(6):
        field = viscosity if f == 5 else adjoint.at[f]
        for x in range(CX):
            low, high = field[x, 0:1, :], field[x, CY - 1 : CY, :]
            at = slice(f * CX + x, f * CX + x + 1)
            y_two[at, :] = jnp.where(odd_y == 1, high, low)
    results = (own, other, ranks)
    near = lax.axis_index("gy") < lax.axis_size("gy") // 2

    @pl.when(near)
    def _():
        gather(adjoint, viscosity, cell, patch, *results)

    @pl.when(jnp.logical_not(near))
    def _():
        for ref in results:
            ref[...] = jnp.zeros(ref.shape, ref.dtype)


def late_kernel(adjoint, viscosity, cell, patch, *refs):
    near = lax.axis_index("gy") < lax.axis_size("gy") // 2

    @pl.when(near)
    def _():
        for found, result in zip(refs[:3], refs[3:]):
            result[...] = found[...]

    @pl.when(jnp.logical_not(near))
    def _():
        gather(adjoint, viscosity, cell, patch, *refs[3:])


def faces_kernel(adjoint, viscosity, rows, before, x_one, x_two, sent):
    sent[...] = rows[...]
    odd_x = parity("gx")
    x_first, x_second = (1 - odd_x) * (CX - 1), odd_x * (CX - 1)
    for f in range(6):
        field = viscosity if f == 5 else adjoint.at[f]
        x_one[f] = field[x_first]
        x_two[f] = field[x_second]


def gather(adjoint, viscosity, cell, patch, own, other, ranks):
    cells = cell[...]
    patches = slot_group(patch[...])
    row = cells >> 8
    span = cells & (CZ - 1)
    span_hot = one_hot(CZ, span, BF16)
    row_hot = lax.broadcasted_iota(jnp.int32, (ROWS, FACES), 0) == row
    values = []
    for f in range(6):
        field = (viscosity[...] if f == 5 else adjoint[f]).reshape(ROWS, CZ)
        both = dot(jnp.concatenate(split(field), axis=0), span_hot)
        found = both[:ROWS] + both[ROWS:]
        values.append(jnp.sum(jnp.where(row_hot, found, 0.0), axis=0, keepdims=True))

    hot = one_hot(PATCHES, patches, F32)
    pieces = FACES // 128
    stacked = jnp.concatenate([hot[:, b * 128 : (b + 1) * 128] for b in range(pieces)], axis=0)
    stacked = stacked.astype(BF16)
    upto = (
        lax.broadcasted_iota(jnp.int32, (128, 256), 0)
        <= lax.broadcasted_iota(jnp.int32, (128, 256), 1)
    )
    counts = dot(stacked, jnp.where(upto, 1.0, 0.0).astype(BF16))
    earlier = jnp.zeros((PATCHES, 128), F32)
    found_ranks = []
    for b in range(pieces):
        mine = slice(b * PATCHES, (b + 1) * PATCHES)
        piece = hot[:, b * 128 : (b + 1) * 128]
        found_ranks.append(
            jnp.sum(piece * (counts[mine, :128] + earlier), axis=0, keepdims=True) - 1.0
        )
        earlier = earlier + counts[mine, 128:]
    rank = jnp.concatenate(found_ranks, axis=1).astype(jnp.int32)
    ranks[...] = rank

    rank_hot = one_hot(CAP, rank, BF16)
    table = jnp.concatenate(values + [jnp.zeros((2, FACES), F32)], axis=0)
    high, low = split(table)
    both = jnp.concatenate([high.astype(F32), low.astype(F32)], axis=0)
    spread = jnp.concatenate(
        [jnp.where(patches == p, both, 0.0).astype(BF16) for p in range(PATCHES)], axis=0
    )
    placed = dot_t(spread, rank_hot).reshape(PATCHES, 16, CAP)
    slots = placed[:, :8] + placed[:, 8:]
    for p in range(HALF):
        own[p * 6 : (p + 1) * 6, :] = slots[p, :6]
        other[p * 6 : (p + 1) * 6, :] = slots[HALF + p, :6]


def interior(adjoint, viscosity, jacobian, faces, out):
    rows = lax.broadcasted_iota(jnp.int32, (CY, CZ), 0)
    lanes = lax.broadcasted_iota(jnp.int32, (CY, CZ), 1)

    def field_at(f, x):
        return viscosity[x] if f == 5 else adjoint[f, x]

    def neighbours(f, x):
        center = field_at(f, x)
        yield field_at(f, max(x - 1, 0))
        yield field_at(f, min(x + 1, CX - 1))
        yield jnp.where(rows == 0, center, pltpu.roll(center, 1, 0))
        yield jnp.where(rows == CY - 1, center, pltpu.roll(center, CY - 1, 0))
        yield jnp.where(lanes == 0, center, pltpu.roll(center, 1, 1))
        yield jnp.where(lanes == CZ - 1, center, pltpu.roll(center, CZ - 1, 1))

    for x in range(CX):
        visc = viscosity[x]
        weights = [0.5 * (visc + other) for other in neighbours(5, x)]
        for f in range(5):
            center = adjoint[f, x]
            total = jnp.zeros((CY, CZ), F32)
            for weight, other in zip(weights, neighbours(f, x)):
                total = total + weight * (other - center)
            for g in range(5):
                total = total + jacobian[f, g] * adjoint[g, x]
            out[f, x] = center + time_step * total


def stencil_kernel(
    adjoint, viscosity, base, x_one, x_two, y_one, y_two, z_one, after, out
):
    def sides(axis, one, two):
        odd, place = parity(axis) == 1, lax.axis_index(axis)
        has_before = jnp.where(place > 0, 1.0, 0.0)
        has_after = jnp.where(place < lax.axis_size(axis) - 1, 1.0, 0.0)
        return jnp.where(odd, one, two) * has_before, jnp.where(odd, two, one) * has_after

    y_sides = sides("gy", y_one[...], y_two[...])
    x_visc = sides("gx", x_one[5], x_two[5])
    side = jnp.transpose(z_one[4 * PROF : 4 * PROF + 8, :])
    lane = (1 - parity("gz")) * (CZ - 1)
    lanes = lax.broadcasted_iota(jnp.int32, (ROWS, CZ), 1)
    visc = viscosity[...].reshape(ROWS, CZ)
    at_edge = jnp.where(lanes == lane, 0.5 * (visc + side[:, 5:6]), 0.0)
    for f in range(5):
        value = adjoint[f].reshape(ROWS, CZ)
        edge = time_step * (at_edge * (side[:, f : f + 1] - value))
        out[f] = base[f] + edge.reshape(CX, CY, CZ)
        for x, beside, other in zip((0, CX - 1), sides("gx", x_one[f], x_two[f]), x_visc):
            weight = 0.5 * (viscosity[x] + other)
            out[f, x] = out[f, x] + time_step * (weight * (beside - adjoint[f, x]))
        for x in range(CX):
            for row, beside in zip((0, CY - 1), y_sides):
                at = slice(row, row + 1)
                other = beside[5 * CX + x : 5 * CX + x + 1]
                weight = 0.5 * (viscosity[x, at, :] + other)
                here = beside[f * CX + x : f * CX + x + 1] - adjoint[f, x, at, :]
                out[f, x, at, :] = out[f, x, at, :] + time_step * (weight * here)


def wide(matrix):
    high, low = split(matrix)
    return jnp.concatenate([high, low, high], axis=1)


def product(left, right):
    high, low = split(right)
    return dot(left, jnp.concatenate([high, high, low], axis=0))


def join_kernel(first, second, third, fourth, edge, joined):
    for at, block in enumerate((first, second, third, fourth)):
        joined[at * PROF : (at + 1) * PROF, :] = block[0, :PROF, :]
    place = lax.axis_index("gz")
    inner = (place ^ (place >> 1)) & 1 == 1
    nearer = (place >> 2) & 1 == (place >> 1) & 1
    passed = jnp.where(nearer, second[0, PROF:, :], fourth[0, PROF:, :])
    joined[4 * PROF : 4 * PROF + 8, :] = edge[...]
    joined[4 * PROF + 8 :, :] = jnp.where(inner, first[0, PROF:, :], passed)


def solve_kernel(mine, theirs, rows, lift, readout, *refs):
    solved = refs[-1]
    inverse = [
        ref[at * PROF : (at + 1) * PROF, :] for ref in (mine, theirs) for at in range(HALF // 2)
    ]
    read = wide(jnp.concatenate([readout[...], jnp.zeros((3, PROF), F32)], axis=0))
    spread = wide(lift[...])
    inverses = [wide(inverse[p]) for p in range(HALF)]
    folded = [wide(product(read, inverse[p])) for p in range(HALF)]
    rows = [rows[p * 6 : (p + 1) * 6, :] for p in range(HALF)]
    forcing = [product(spread, r) for r in rows]
    damping = [0.5 * r[5:6] for r in rows]
    right = forcing
    for sweep in range(ITERS - 1):
        profile = [product(w, r) for w, r in zip(inverses, right)]
        right = [g - d * jnp.tanh(q) for g, d, q in zip(forcing, damping, profile)]
    for p in range(HALF):
        result = product(folded[p], right[p])
        for f in range(5):
            solved[f * HALF + p : f * HALF + p + 1, :] = result[f : f + 1]
    solved[5 * HALF :, :] = theirs[4 * PROF + 8 :, :]


def scatter_kernel(
    solved_own,
    returned,
    cell,
    patch,
    ranks,
    partial,
    adjoint,
    viscosity,
    updated,
    shear,
):
    parts = (solved_own[: 5 * HALF, :], returned[: 5 * HALF, :])
    result = jnp.concatenate(parts, axis=0)
    rank_hot = one_hot(CAP, ranks[...], BF16)
    back = dot(
        jnp.concatenate(split(result), axis=1), jnp.concatenate([rank_hot, rank_hot], axis=0)
    )
    patches = slot_group(patch[...])
    numbers = lax.broadcasted_iota(jnp.int32, (HALF, FACES), 0)
    kept = [numbers == patches, numbers + HALF == patches]
    walls = []
    for f in range(5):
        parts = [back[at + f * HALF : at + (f + 1) * HALF] for at in (0, 5 * HALF)]
        both = jnp.where(kept[0], parts[0], 0.0) + jnp.where(kept[1], parts[1], 0.0)
        walls.append(jnp.sum(both, axis=0, keepdims=True))
    wall = jnp.concatenate(walls + [jnp.zeros((3, FACES), F32)], axis=0)
    shear[...] = wall[:5]

    side = jnp.transpose(returned[5 * HALF :, :])
    lane = parity("gz") * (CZ - 1)
    lanes = lax.broadcasted_iota(jnp.int32, (ROWS, CZ), 1)
    visc = viscosity[...].reshape(ROWS, CZ)
    at_edge = jnp.where(lanes == lane, 0.5 * (visc + side[:, 5:6]), 0.0)
    cells = cell[...]
    span_hot = one_hot(CZ, cells & (CZ - 1), BF16)
    row_hot = lax.broadcasted_iota(jnp.int32, (ROWS, FACES), 0) == (cells >> 8)
    high = wall.astype(BF16).astype(F32)
    low = wall - high
    for f in range(5):
        spread = [jnp.where(row_hot, part[f : f + 1], 0.0).astype(BF16) for part in (high, low)]
        both = dot_t(jnp.concatenate(spread, axis=0), span_hot)
        source = both[:ROWS] + both[ROWS:]
        value = adjoint[f].reshape(ROWS, CZ)
        edge = at_edge * (side[:, f : f + 1] - value)
        updated[f] = partial[f] + (time_step * (source + edge)).reshape(CX, CY, CZ)


def swapped(array, axis, partner):
    return lax.ppermute(array, axis, [(i, partner(i)) for i in range(lax.axis_size(axis))])


def first_side(array, axis):
    return swapped(array, axis, lambda i: i ^ 1)


def second_side(array, axis):
    size = lax.axis_size(axis)
    return swapped(array, axis, lambda i: (i + 1 if i % 2 else i - 1) % size)


def shape(*dims, dtype=F32):
    return jax.ShapeDtypeStruct(dims, dtype)


def body(
    adjoint, viscosity, flux_jacobian, face_cell, face_patch, wall_inverse, lift_matrix, readout
):
    cell = face_cell.reshape(1, FACES)
    patch = face_patch.reshape(1, FACES)
    face_x, face_y, face_z = shape(6, CY, CZ), shape(6 * CX, CZ), shape(8, ROWS)
    slots, numbers = shape(HALF * 6, CAP), shape(1, FACES, dtype=jnp.int32)
    arrays = [adjoint, viscosity, cell, patch, wall_inverse]
    package = shape(1, PROF + 8, PROF)
    adjoint, viscosity, cell, patch, package, y_one, z_one = pl.pallas_call(
        load_kernel,
        out_shape=tuple(shape(*a.shape, dtype=a.dtype) for a in arrays[:4])
        + (package, face_y, face_z),
        in_specs=[HBM] * 5,
        out_specs=[VMEM] * 7,
        scratch_shapes=[pltpu.SemaphoreType.DMA((5,))],
        compiler_params=PARAMS,
        name="load",
    )(*[pltpu.with_memory_space_constraint(a, pltpu.HBM) for a in arrays])
    blocks = [package]
    for step in range(1, 4):
        blocks.append(swapped(package, "gz", lambda i: i ^ (4 * step)))
    mine = pl.pallas_call(
        join_kernel,
        out_shape=shape(4 * PROF + 16, PROF),
        in_specs=[VMEM] * 5,
        out_specs=VMEM,
        compiler_params=PARAMS,
        name="join",
    )(*blocks, z_one)
    theirs = swapped(mine, "gz", lambda i: i ^ 1)
    fields = (adjoint, viscosity, cell, patch)
    gathered = (slots, slots, numbers)
    y_one = first_side(y_one, "gy")
    y_two, *found = pl.pallas_call(
        early_kernel,
        out_shape=(face_y,) + gathered,
        in_specs=[VMEM] * 4 + [ANY] * 2,
        out_specs=[VMEM] * 4,
        compiler_params=PARAMS,
        name="early_gather",
    )(*fields, y_one, y_one)
    y_two = second_side(y_two, "gy")
    own, other, ranks = pl.pallas_call(
        late_kernel,
        out_shape=gathered,
        in_specs=[VMEM] * 7,
        out_specs=[VMEM] * 3,
        compiler_params=PARAMS,
        cost_estimate=LONG,
        name="late_gather",
    )(*fields, *found)
    x_one, x_two, other = pl.pallas_call(
        faces_kernel,
        out_shape=(face_x, face_x, slots),
        in_specs=[VMEM, VMEM, VMEM, ANY],
        out_specs=[VMEM] * 3,
        compiler_params=PARAMS,
        cost_estimate=LONG,
        name="faces",
    )(adjoint, viscosity, other, y_two)
    arrived = swapped(other, "gz", lambda i: i ^ 2)
    def solve(rows, *after):
        return pl.pallas_call(
            solve_kernel,
            out_shape=shape(5 * HALF + 8, CAP),
            in_specs=[VMEM] * 5 + [ANY] * len(after),
            out_specs=VMEM,
            compiler_params=PARAMS,
            cost_estimate=LONG,
            name="solve",
        )(mine, theirs, rows, lift_matrix, readout, *after)

    base = pl.pallas_call(
        interior,
        out_shape=shape(5, CX, CY, CZ),
        in_specs=[VMEM, VMEM, SMEM, ANY],
        out_specs=VMEM,
        compiler_params=PARAMS,
        cost_estimate=SHORT,
        name="interior",
    )(adjoint, viscosity, flux_jacobian, x_one)
    solved_arrived = solve(arrived, base)
    returned = swapped(solved_arrived, "gz", lambda i: i ^ 2)
    solved_own = solve(own, solved_arrived)
    partial = pl.pallas_call(
        stencil_kernel,
        out_shape=shape(5, CX, CY, CZ),
        in_specs=[VMEM] * 8 + [ANY],
        out_specs=VMEM,
        compiler_params=PARAMS,
        cost_estimate=LONG,
        name="stencil",
    )(
        adjoint,
        viscosity,
        base,
        first_side(x_one, "gx"),
        second_side(x_two, "gx"),
        y_one,
        y_two,
        theirs,
        solved_own,
    )
    return pl.pallas_call(
        scatter_kernel,
        out_shape=(shape(5, CX, CY, CZ), shape(5, FACES)),
        in_specs=[VMEM] * 8,
        out_specs=[VMEM] * 2,
        compiler_params=PARAMS,
        name="scatter",
    )(
        solved_own,
        returned,
        cell,
        patch,
        ranks,
        partial,
        adjoint,
        viscosity,
    )


def solution(mesh):
    in_specs = (
        P(None, "gx", "gy", "gz"),
        P("gx", "gy", "gz"),
        P(),
        P(("gx", "gy", "gz")),
        P(("gx", "gy", "gz"), None),
        P(("gx", "gy", "gz"), None, None),
        P(),
        P(),
    )
    out_specs = (P(None, "gx", "gy", "gz"), P(None, ("gx", "gy", "gz")))
    return jax.shard_map(body, mesh=mesh, in_specs=in_specs, out_specs=out_specs, check_vma=False)
```

```python
import functools

import jax
import jax.numpy as jnp
from jax import lax
from jax.experimental import pallas as pl
from jax.experimental.pallas import tpu as pltpu
from jax.sharding import PartitionSpec as P

CX = 4
CY = 32
CZ = 256
FACES = 1024
ROWS = CX * CY
PATCHES = 16
HALF = 8
CAP = 128
PROF = 128
ITERS = 6

time_step = 0.08

F32 = jnp.float32
BF16 = jnp.bfloat16
VMEM = pl.BlockSpec(memory_space=pltpu.VMEM)
HBM = pl.BlockSpec(memory_space=pltpu.HBM)
ANY = pl.BlockSpec(memory_space=pl.ANY)
SMEM = pl.BlockSpec(memory_space=pltpu.SMEM)
LONG = pl.CostEstimate(flops=20_000_000_000, bytes_accessed=60_000_000, transcendentals=0)
SHORT = pl.CostEstimate(flops=1000, bytes_accessed=1000, transcendentals=0)
PARAMS = pltpu.CompilerParams(vmem_limit_bytes=48 * 1024 * 1024)


def split(x):
    high = x.astype(BF16)
    low = (x - high.astype(F32)).astype(BF16)
    return high, low


def dot(a, b):
    return jnp.dot(a, b, preferred_element_type=F32)


def dot_t(a, b):
    return lax.dot_general(a, b, (((1,), (1,)), ((), ())), preferred_element_type=F32)


def one_hot(count, index, dtype):
    numbers = lax.broadcasted_iota(jnp.int32, (count, index.shape[-1]), 0)
    return jnp.where(numbers == index, 1.0, 0.0).astype(dtype)


def parity(axis):
    return lax.axis_index(axis) & 1


def slot_group(patches):
    apart = patches ^ lax.axis_index("gz")
    return ((apart >> 1) & 1) * HALF + (apart & 1) * (HALF // 2) + (apart >> 2)


def load_kernel(
    adjoint_hbm,
    viscosity_hbm,
    cell_hbm,
    patch_hbm,
    inverse_hbm,
    adjoint,
    viscosity,
    cell,
    patch,
    package,
    y_one,
    z_one,
    arrivals,
):
    pairs = (
        (viscosity_hbm, viscosity),
        (adjoint_hbm, adjoint),
        (cell_hbm, cell),
        (patch_hbm, patch),
        (inverse_hbm, package.at[:, :PROF]),
    )
    copies = [
        pltpu.make_async_copy(source, target, arrivals.at[at])
        for at, (source, target) in enumerate(pairs)
    ]
    for copy in copies:
        copy.start()
    copies[0].wait()
    copies[1].wait()
    odd_y = parity("gy")
    for f in range(6):
        field = viscosity if f == 5 else adjoint.at[f]
        for x in range(CX):
            low, high = field[x, 0:1, :], field[x, CY - 1 : CY, :]
            at = slice(f * CX + x, f * CX + x + 1)
            y_one[at, :] = jnp.where(odd_y == 1, low, high)
    columns = lax.broadcasted_iota(jnp.int32, (ROWS, 128), 1)
    z_low = z_high = jnp.zeros((ROWS, 128), F32)
    for f in range(6):
        field = (viscosity[...] if f == 5 else adjoint[f]).reshape(ROWS, CZ)
        z_low = jnp.where(columns == f, field[:, 0:1], z_low)
        z_high = jnp.where(columns == f, field[:, CZ - 1 : CZ], z_high)
    z_low, z_high = jnp.transpose(z_low)[:8], jnp.transpose(z_high)[:8]
    odd_z = parity("gz") == 1
    z_one[...] = jnp.where(odd_z, z_low, z_high)
    package[0, PROF:, :] = jnp.where(odd_z, z_high, z_low)
    for copy in copies[2:]:
        copy.wait()


def early_kernel(
    adjoint, viscosity, cell, patch, before, joined, y_two, own, other, ranks
):
    odd_y = parity("gy")
    for f in range(6):
        field = viscosity if f == 5 else adjoint.at[f]
        for x in range(CX):
            low, high = field[x, 0:1, :], field[x, CY - 1 : CY, :]
            at = slice(f * CX + x, f * CX + x + 1)
            y_two[at, :] = jnp.where(odd_y == 1, high, low)
    results = (own, other, ranks)
    near = lax.axis_index("gy") < lax.axis_size("gy") // 2

    @pl.when(near)
    def _():
        gather(adjoint, viscosity, cell, patch, *results)

    @pl.when(jnp.logical_not(near))
    def _():
        for ref in results:
            ref[...] = jnp.zeros(ref.shape, ref.dtype)


def late_kernel(adjoint, viscosity, cell, patch, *refs):
    near = lax.axis_index("gy") < lax.axis_size("gy") // 2

    @pl.when(near)
    def _():
        for found, result in zip(refs[:3], refs[3:]):
            result[...] = found[...]

    @pl.when(jnp.logical_not(near))
    def _():
        gather(adjoint, viscosity, cell, patch, *refs[3:])


def faces_kernel(adjoint, viscosity, rows, before, base, x_one, x_two, sent):
    sent[...] = rows[...]
    odd_x = parity("gx")
    x_first, x_second = (1 - odd_x) * (CX - 1), odd_x * (CX - 1)
    for f in range(6):
        field = viscosity if f == 5 else adjoint.at[f]
        x_one[f] = field[x_first]
        x_two[f] = field[x_second]


def gather(adjoint, viscosity, cell, patch, own, other, ranks):
    cells = cell[...]
    patches = slot_group(patch[...])
    row = cells >> 8
    span = cells & (CZ - 1)
    span_hot = one_hot(CZ, span, BF16)
    row_hot = lax.broadcasted_iota(jnp.int32, (ROWS, FACES), 0) == row
    values = []
    for f in range(6):
        field = (viscosity[...] if f == 5 else adjoint[f]).reshape(ROWS, CZ)
        both = dot(jnp.concatenate(split(field), axis=0), span_hot)
        found = both[:ROWS] + both[ROWS:]
        values.append(jnp.sum(jnp.where(row_hot, found, 0.0), axis=0, keepdims=True))

    hot = one_hot(PATCHES, patches, F32)
    pieces = FACES // 128
    stacked = jnp.concatenate([hot[:, b * 128 : (b + 1) * 128] for b in range(pieces)], axis=0)
    stacked = stacked.astype(BF16)
    upto = (
        lax.broadcasted_iota(jnp.int32, (128, 256), 0)
        <= lax.broadcasted_iota(jnp.int32, (128, 256), 1)
    )
    counts = dot(stacked, jnp.where(upto, 1.0, 0.0).astype(BF16))
    earlier = jnp.zeros((PATCHES, 128), F32)
    found_ranks = []
    for b in range(pieces):
        mine = slice(b * PATCHES, (b + 1) * PATCHES)
        piece = hot[:, b * 128 : (b + 1) * 128]
        found_ranks.append(
            jnp.sum(piece * (counts[mine, :128] + earlier), axis=0, keepdims=True) - 1.0
        )
        earlier = earlier + counts[mine, 128:]
    rank = jnp.concatenate(found_ranks, axis=1).astype(jnp.int32)
    ranks[...] = rank

    rank_hot = one_hot(CAP, rank, BF16)
    table = jnp.concatenate(values + [jnp.zeros((2, FACES), F32)], axis=0)
    high, low = split(table)
    both = jnp.concatenate([high.astype(F32), low.astype(F32)], axis=0)
    spread = jnp.concatenate(
        [jnp.where(patches == p, both, 0.0).astype(BF16) for p in range(PATCHES)], axis=0
    )
    placed = dot_t(spread, rank_hot).reshape(PATCHES, 16, CAP)
    slots = placed[:, :8] + placed[:, 8:]
    for p in range(HALF):
        own[p * 6 : (p + 1) * 6, :] = slots[p, :6]
        other[p * 6 : (p + 1) * 6, :] = slots[HALF + p, :6]


def interior(adjoint, viscosity, jacobian, faces, out):
    rows = lax.broadcasted_iota(jnp.int32, (CY, CZ), 0)
    lanes = lax.broadcasted_iota(jnp.int32, (CY, CZ), 1)

    def field_at(f, x):
        return viscosity[x] if f == 5 else adjoint[f, x]

    def neighbours(f, x):
        center = field_at(f, x)
        yield field_at(f, max(x - 1, 0))
        yield field_at(f, min(x + 1, CX - 1))
        yield jnp.where(rows == 0, center, pltpu.roll(center, 1, 0))
        yield jnp.where(rows == CY - 1, center, pltpu.roll(center, CY - 1, 0))
        yield jnp.where(lanes == 0, center, pltpu.roll(center, 1, 1))
        yield jnp.where(lanes == CZ - 1, center, pltpu.roll(center, CZ - 1, 1))

    for x in range(CX):
        visc = viscosity[x]
        weights = [0.5 * (visc + other) for other in neighbours(5, x)]
        for f in range(5):
            center = adjoint[f, x]
            total = jnp.zeros((CY, CZ), F32)
            for weight, other in zip(weights, neighbours(f, x)):
                total = total + weight * (other - center)
            for g in range(5):
                total = total + jacobian[f, g] * adjoint[g, x]
            out[f, x] = center + time_step * total


def stencil_kernel(
    adjoint, viscosity, base, x_one, x_two, y_one, y_two, z_one, after, out
):
    def sides(axis, one, two):
        odd, place = parity(axis) == 1, lax.axis_index(axis)
        has_before = jnp.where(place > 0, 1.0, 0.0)
        has_after = jnp.where(place < lax.axis_size(axis) - 1, 1.0, 0.0)
        return jnp.where(odd, one, two) * has_before, jnp.where(odd, two, one) * has_after

    y_sides = sides("gy", y_one[...], y_two[...])
    x_visc = sides("gx", x_one[5], x_two[5])
    side = jnp.transpose(z_one[4 * PROF : 4 * PROF + 8, :])
    lane = (1 - parity("gz")) * (CZ - 1)
    lanes = lax.broadcasted_iota(jnp.int32, (ROWS, CZ), 1)
    visc = viscosity[...].reshape(ROWS, CZ)
    at_edge = jnp.where(lanes == lane, 0.5 * (visc + side[:, 5:6]), 0.0)
    for f in range(5):
        value = adjoint[f].reshape(ROWS, CZ)
        edge = time_step * (at_edge * (side[:, f : f + 1] - value))
        out[f] = base[f] + edge.reshape(CX, CY, CZ)
        for x, beside, other in zip((0, CX - 1), sides("gx", x_one[f], x_two[f]), x_visc):
            weight = 0.5 * (viscosity[x] + other)
            out[f, x] = out[f, x] + time_step * (weight * (beside - adjoint[f, x]))
        for x in range(CX):
            for row, beside in zip((0, CY - 1), y_sides):
                at = slice(row, row + 1)
                other = beside[5 * CX + x : 5 * CX + x + 1]
                weight = 0.5 * (viscosity[x, at, :] + other)
                here = beside[f * CX + x : f * CX + x + 1] - adjoint[f, x, at, :]
                out[f, x, at, :] = out[f, x, at, :] + time_step * (weight * here)


def wide(matrix):
    high, low = split(matrix)
    return jnp.concatenate([high, low, high], axis=1)


def product(left, right):
    high, low = split(right)
    return dot(left, jnp.concatenate([high, high, low], axis=0))


def join_kernel(first, second, third, fourth, edge, joined):
    for at, block in enumerate((first, second, third, fourth)):
        joined[at * PROF : (at + 1) * PROF, :] = block[0, :PROF, :]
    place = lax.axis_index("gz")
    inner = (place ^ (place >> 1)) & 1 == 1
    nearer = (place >> 2) & 1 == (place >> 1) & 1
    passed = jnp.where(nearer, second[0, PROF:, :], fourth[0, PROF:, :])
    joined[4 * PROF : 4 * PROF + 8, :] = edge[...]
    joined[4 * PROF + 8 :, :] = jnp.where(inner, first[0, PROF:, :], passed)


def solve_kernel(mine, theirs, rows, lift, readout, *refs):
    solved = refs[-1]
    inverse = [
        ref[at * PROF : (at + 1) * PROF, :] for ref in (mine, theirs) for at in range(HALF // 2)
    ]
    read = wide(jnp.concatenate([readout[...], jnp.zeros((3, PROF), F32)], axis=0))
    spread = wide(lift[...])
    inverses = [wide(inverse[p]) for p in range(HALF)]
    folded = [wide(product(read, inverse[p])) for p in range(HALF)]
    rows = [rows[p * 6 : (p + 1) * 6, :] for p in range(HALF)]
    forcing = [product(spread, r) for r in rows]
    damping = [0.5 * r[5:6] for r in rows]
    right = forcing
    for sweep in range(ITERS - 1):
        profile = [product(w, r) for w, r in zip(inverses, right)]
        right = [g - d * jnp.tanh(q) for g, d, q in zip(forcing, damping, profile)]
    for p in range(HALF):
        result = product(folded[p], right[p])
        for f in range(5):
            solved[f * HALF + p : f * HALF + p + 1, :] = result[f : f + 1]
    solved[5 * HALF :, :] = theirs[4 * PROF + 8 :, :]


def scatter_kernel(
    solved_own,
    returned,
    cell,
    patch,
    ranks,
    partial,
    adjoint,
    viscosity,
    updated,
    shear,
):
    parts = (solved_own[: 5 * HALF, :], returned[: 5 * HALF, :])
    result = jnp.concatenate(parts, axis=0)
    rank_hot = one_hot(CAP, ranks[...], BF16)
    back = dot(
        jnp.concatenate(split(result), axis=1), jnp.concatenate([rank_hot, rank_hot], axis=0)
    )
    patches = slot_group(patch[...])
    numbers = lax.broadcasted_iota(jnp.int32, (HALF, FACES), 0)
    kept = [numbers == patches, numbers + HALF == patches]
    walls = []
    for f in range(5):
        parts = [back[at + f * HALF : at + (f + 1) * HALF] for at in (0, 5 * HALF)]
        both = jnp.where(kept[0], parts[0], 0.0) + jnp.where(kept[1], parts[1], 0.0)
        walls.append(jnp.sum(both, axis=0, keepdims=True))
    wall = jnp.concatenate(walls + [jnp.zeros((3, FACES), F32)], axis=0)
    shear[...] = wall[:5]

    side = jnp.transpose(returned[5 * HALF :, :])
    lane = parity("gz") * (CZ - 1)
    lanes = lax.broadcasted_iota(jnp.int32, (ROWS, CZ), 1)
    visc = viscosity[...].reshape(ROWS, CZ)
    at_edge = jnp.where(lanes == lane, 0.5 * (visc + side[:, 5:6]), 0.0)
    cells = cell[...]
    span_hot = one_hot(CZ, cells & (CZ - 1), BF16)
    row_hot = lax.broadcasted_iota(jnp.int32, (ROWS, FACES), 0) == (cells >> 8)
    high = wall.astype(BF16).astype(F32)
    low = wall - high
    for f in range(5):
        spread = [jnp.where(row_hot, part[f : f + 1], 0.0).astype(BF16) for part in (high, low)]
        both = dot_t(jnp.concatenate(spread, axis=0), span_hot)
        source = both[:ROWS] + both[ROWS:]
        value = adjoint[f].reshape(ROWS, CZ)
        edge = at_edge * (side[:, f : f + 1] - value)
        updated[f] = partial[f] + (time_step * (source + edge)).reshape(CX, CY, CZ)


def swapped(array, axis, partner):
    return lax.ppermute(array, axis, [(i, partner(i)) for i in range(lax.axis_size(axis))])


def first_side(array, axis):
    return swapped(array, axis, lambda i: i ^ 1)


def second_side(array, axis):
    size = lax.axis_size(axis)
    return swapped(array, axis, lambda i: (i + 1 if i % 2 else i - 1) % size)


def shape(*dims, dtype=F32):
    return jax.ShapeDtypeStruct(dims, dtype)


def body(
    adjoint, viscosity, flux_jacobian, face_cell, face_patch, wall_inverse, lift_matrix, readout
):
    cell = face_cell.reshape(1, FACES)
    patch = face_patch.reshape(1, FACES)
    face_x, face_y, face_z = shape(6, CY, CZ), shape(6 * CX, CZ), shape(8, ROWS)
    slots, numbers = shape(HALF * 6, CAP), shape(1, FACES, dtype=jnp.int32)
    arrays = [adjoint, viscosity, cell, patch, wall_inverse]
    package = shape(1, PROF + 8, PROF)
    adjoint, viscosity, cell, patch, package, y_one, z_one = pl.pallas_call(
        load_kernel,
        out_shape=tuple(shape(*a.shape, dtype=a.dtype) for a in arrays[:4])
        + (package, face_y, face_z),
        in_specs=[HBM] * 5,
        out_specs=[VMEM] * 7,
        scratch_shapes=[pltpu.SemaphoreType.DMA((5,))],
        compiler_params=PARAMS,
        name="load",
    )(*[pltpu.with_memory_space_constraint(a, pltpu.HBM) for a in arrays])
    blocks = [package]
    for step in range(1, 4):
        blocks.append(swapped(package, "gz", lambda i: i ^ (4 * step)))
    mine = pl.pallas_call(
        join_kernel,
        out_shape=shape(4 * PROF + 16, PROF),
        in_specs=[VMEM] * 5,
        out_specs=VMEM,
        compiler_params=PARAMS,
        name="join",
    )(*blocks, z_one)
    theirs = swapped(mine, "gz", lambda i: i ^ 1)
    fields = (adjoint, viscosity, cell, patch)
    gathered = (slots, slots, numbers)
    y_one = first_side(y_one, "gy")
    y_two, *found = pl.pallas_call(
        early_kernel,
        out_shape=(face_y,) + gathered,
        in_specs=[VMEM] * 4 + [ANY] * 2,
        out_specs=[VMEM] * 4,
        compiler_params=PARAMS,
        name="early_gather",
    )(*fields, y_one, y_one)
    y_two = second_side(y_two, "gy")
    own, other, ranks = pl.pallas_call(
        late_kernel,
        out_shape=gathered,
        in_specs=[VMEM] * 7,
        out_specs=[VMEM] * 3,
        compiler_params=PARAMS,
        cost_estimate=LONG,
        name="late_gather",
    )(*fields, *found)
    base = pl.pallas_call(
        interior,
        out_shape=shape(5, CX, CY, CZ),
        in_specs=[VMEM, VMEM, SMEM, ANY],
        out_specs=VMEM,
        compiler_params=PARAMS,
        cost_estimate=SHORT,
        name="interior",
    )(adjoint, viscosity, flux_jacobian, mine)
    x_one, x_two, other = pl.pallas_call(
        faces_kernel,
        out_shape=(face_x, face_x, slots),
        in_specs=[VMEM, VMEM, VMEM, ANY, ANY],
        out_specs=[VMEM] * 3,
        compiler_params=PARAMS,
        cost_estimate=LONG,
        name="faces",
    )(adjoint, viscosity, other, y_two, base)
    arrived = swapped(other, "gz", lambda i: i ^ 2)
    def solve(rows, *after):
        return pl.pallas_call(
            solve_kernel,
            out_shape=shape(5 * HALF + 8, CAP),
            in_specs=[VMEM] * 5 + [ANY] * len(after),
            out_specs=VMEM,
            compiler_params=PARAMS,
            cost_estimate=LONG,
            name="solve",
        )(mine, theirs, rows, lift_matrix, readout, *after)

    solved_arrived = solve(arrived)
    returned = swapped(solved_arrived, "gz", lambda i: i ^ 2)
    solved_own = solve(own, solved_arrived)
    partial = pl.pallas_call(
        stencil_kernel,
        out_shape=shape(5, CX, CY, CZ),
        in_specs=[VMEM] * 8 + [ANY],
        out_specs=VMEM,
        compiler_params=PARAMS,
        cost_estimate=LONG,
        name="stencil",
    )(
        adjoint,
        viscosity,
        base,
        first_side(x_one, "gx"),
        second_side(x_two, "gx"),
        y_one,
        y_two,
        theirs,
        solved_own,
    )
    return pl.pallas_call(
        scatter_kernel,
        out_shape=(shape(5, CX, CY, CZ), shape(5, FACES)),
        in_specs=[VMEM] * 8,
        out_specs=[VMEM] * 2,
        compiler_params=PARAMS,
        name="scatter",
    )(
        solved_own,
        returned,
        cell,
        patch,
        ranks,
        partial,
        adjoint,
        viscosity,
    )


def solution(mesh):
    in_specs = (
        P(None, "gx", "gy", "gz"),
        P("gx", "gy", "gz"),
        P(),
        P(("gx", "gy", "gz")),
        P(("gx", "gy", "gz"), None),
        P(("gx", "gy", "gz"), None, None),
        P(),
        P(),
    )
    out_specs = (P(None, "gx", "gy", "gz"), P(None, ("gx", "gy", "gz")))
    return jax.shard_map(body, mesh=mesh, in_specs=in_specs, out_specs=out_specs, check_vma=False)
```

```python
import functools

import jax
import jax.numpy as jnp
from jax import lax
from jax.experimental import pallas as pl
from jax.experimental.pallas import tpu as pltpu
from jax.sharding import PartitionSpec as P

CX = 4
CY = 32
CZ = 256
FACES = 1024
ROWS = CX * CY
PATCHES = 16
HALF = 8
CAP = 128
PROF = 128
ITERS = 6

time_step = 0.08

F32 = jnp.float32
BF16 = jnp.bfloat16
VMEM = pl.BlockSpec(memory_space=pltpu.VMEM)
HBM = pl.BlockSpec(memory_space=pltpu.HBM)
ANY = pl.BlockSpec(memory_space=pl.ANY)
SMEM = pl.BlockSpec(memory_space=pltpu.SMEM)
LONG = pl.CostEstimate(flops=20_000_000_000, bytes_accessed=60_000_000, transcendentals=0)
SHORT = pl.CostEstimate(flops=1000, bytes_accessed=1000, transcendentals=0)
PARAMS = pltpu.CompilerParams(vmem_limit_bytes=48 * 1024 * 1024)


def split(x):
    high = x.astype(BF16)
    low = (x - high.astype(F32)).astype(BF16)
    return high, low


def dot(a, b):
    return jnp.dot(a, b, preferred_element_type=F32)


def dot_t(a, b):
    return lax.dot_general(a, b, (((1,), (1,)), ((), ())), preferred_element_type=F32)


def one_hot(count, index, dtype):
    numbers = lax.broadcasted_iota(jnp.int32, (count, index.shape[-1]), 0)
    return jnp.where(numbers == index, 1.0, 0.0).astype(dtype)


def parity(axis):
    return lax.axis_index(axis) & 1


def slot_group(patches):
    apart = patches ^ lax.axis_index("gz")
    return ((apart >> 1) & 1) * HALF + (apart & 1) * (HALF // 2) + (apart >> 2)


def z_face(adjoint, viscosity, far):
    columns = lax.broadcasted_iota(jnp.int32, (ROWS, 128), 1)
    face = jnp.zeros((ROWS, 128), F32)
    for f in range(6):
        field = (viscosity[...] if f == 5 else adjoint[f]).reshape(ROWS, CZ)
        edge = jnp.where(far == 1, field[:, CZ - 1 : CZ], field[:, 0:1])
        face = jnp.where(columns == f, edge, face)
    return jnp.transpose(face)[:8]


def load_kernel(
    adjoint_hbm,
    viscosity_hbm,
    cell_hbm,
    patch_hbm,
    inverse_hbm,
    adjoint,
    viscosity,
    cell,
    patch,
    package,
    y_one,
    arrivals,
):
    pairs = (
        (viscosity_hbm, viscosity),
        (adjoint_hbm, adjoint),
        (cell_hbm, cell),
        (patch_hbm, patch),
        (inverse_hbm, package.at[:, :PROF]),
    )
    copies = [
        pltpu.make_async_copy(source, target, arrivals.at[at])
        for at, (source, target) in enumerate(pairs)
    ]
    for copy in copies:
        copy.start()
    copies[0].wait()
    copies[1].wait()
    odd_y = parity("gy")
    for f in range(6):
        field = viscosity if f == 5 else adjoint.at[f]
        for x in range(CX):
            low, high = field[x, 0:1, :], field[x, CY - 1 : CY, :]
            at = slice(f * CX + x, f * CX + x + 1)
            y_one[at, :] = jnp.where(odd_y == 1, low, high)
    package[0, PROF:, :] = z_face(adjoint, viscosity, parity("gz"))
    for copy in copies[2:]:
        copy.wait()


def early_kernel(
    adjoint, viscosity, cell, patch, before, joined, y_two, own, other, ranks, z_one
):
    odd_y = parity("gy")
    for f in range(6):
        field = viscosity if f == 5 else adjoint.at[f]
        for x in range(CX):
            low, high = field[x, 0:1, :], field[x, CY - 1 : CY, :]
            at = slice(f * CX + x, f * CX + x + 1)
            y_two[at, :] = jnp.where(odd_y == 1, high, low)
    results = (own, other, ranks, z_one)
    near = lax.axis_index("gy") < lax.axis_size("gy") // 2

    @pl.when(near)
    def _():
        gather(adjoint, viscosity, cell, patch, *results)

    @pl.when(jnp.logical_not(near))
    def _():
        for ref in results:
            ref[...] = jnp.zeros(ref.shape, ref.dtype)


def late_kernel(adjoint, viscosity, cell, patch, *refs):
    near = lax.axis_index("gy") < lax.axis_size("gy") // 2

    @pl.when(near)
    def _():
        for found, result in zip(refs[:4], refs[4:]):
            result[...] = found[...]

    @pl.when(jnp.logical_not(near))
    def _():
        gather(adjoint, viscosity, cell, patch, *refs[4:])


def faces_kernel(adjoint, viscosity, rows, before, base, x_one, x_two, sent):
    sent[...] = rows[...]
    odd_x = parity("gx")
    x_first, x_second = (1 - odd_x) * (CX - 1), odd_x * (CX - 1)
    for f in range(6):
        field = viscosity if f == 5 else adjoint.at[f]
        x_one[f] = field[x_first]
        x_two[f] = field[x_second]


def gather(adjoint, viscosity, cell, patch, own, other, ranks, z_one):
    z_one[...] = z_face(adjoint, viscosity, 1 - parity("gz"))
    cells = cell[...]
    patches = slot_group(patch[...])
    row = cells >> 8
    span = cells & (CZ - 1)
    span_hot = one_hot(CZ, span, BF16)
    row_hot = lax.broadcasted_iota(jnp.int32, (ROWS, FACES), 0) == row
    values = []
    for f in range(6):
        field = (viscosity[...] if f == 5 else adjoint[f]).reshape(ROWS, CZ)
        both = dot(jnp.concatenate(split(field), axis=0), span_hot)
        found = both[:ROWS] + both[ROWS:]
        values.append(jnp.sum(jnp.where(row_hot, found, 0.0), axis=0, keepdims=True))

    hot = one_hot(PATCHES, patches, F32)
    pieces = FACES // 128
    stacked = jnp.concatenate([hot[:, b * 128 : (b + 1) * 128] for b in range(pieces)], axis=0)
    stacked = stacked.astype(BF16)
    upto = (
        lax.broadcasted_iota(jnp.int32, (128, 256), 0)
        <= lax.broadcasted_iota(jnp.int32, (128, 256), 1)
    )
    counts = dot(stacked, jnp.where(upto, 1.0, 0.0).astype(BF16))
    earlier = jnp.zeros((PATCHES, 128), F32)
    found_ranks = []
    for b in range(pieces):
        mine = slice(b * PATCHES, (b + 1) * PATCHES)
        piece = hot[:, b * 128 : (b + 1) * 128]
        found_ranks.append(
            jnp.sum(piece * (counts[mine, :128] + earlier), axis=0, keepdims=True) - 1.0
        )
        earlier = earlier + counts[mine, 128:]
    rank = jnp.concatenate(found_ranks, axis=1).astype(jnp.int32)
    ranks[...] = rank

    rank_hot = one_hot(CAP, rank, BF16)
    table = jnp.concatenate(values + [jnp.zeros((2, FACES), F32)], axis=0)
    high, low = split(table)
    both = jnp.concatenate([high.astype(F32), low.astype(F32)], axis=0)
    spread = jnp.concatenate(
        [jnp.where(patches == p, both, 0.0).astype(BF16) for p in range(PATCHES)], axis=0
    )
    placed = dot_t(spread, rank_hot).reshape(PATCHES, 16, CAP)
    slots = placed[:, :8] + placed[:, 8:]
    for p in range(HALF):
        own[p * 6 : (p + 1) * 6, :] = slots[p, :6]
        other[p * 6 : (p + 1) * 6, :] = slots[HALF + p, :6]


def interior(adjoint, viscosity, jacobian, faces, out):
    rows = lax.broadcasted_iota(jnp.int32, (CY, CZ), 0)
    lanes = lax.broadcasted_iota(jnp.int32, (CY, CZ), 1)

    def field_at(f, x):
        return viscosity[x] if f == 5 else adjoint[f, x]

    def neighbours(f, x):
        center = field_at(f, x)
        yield field_at(f, max(x - 1, 0))
        yield field_at(f, min(x + 1, CX - 1))
        yield jnp.where(rows == 0, center, pltpu.roll(center, 1, 0))
        yield jnp.where(rows == CY - 1, center, pltpu.roll(center, CY - 1, 0))
        yield jnp.where(lanes == 0, center, pltpu.roll(center, 1, 1))
        yield jnp.where(lanes == CZ - 1, center, pltpu.roll(center, CZ - 1, 1))

    for x in range(CX):
        visc = viscosity[x]
        weights = [0.5 * (visc + other) for other in neighbours(5, x)]
        for f in range(5):
            center = adjoint[f, x]
            total = jnp.zeros((CY, CZ), F32)
            for weight, other in zip(weights, neighbours(f, x)):
                total = total + weight * (other - center)
            for g in range(5):
                total = total + jacobian[f, g] * adjoint[g, x]
            out[f, x] = center + time_step * total


def stencil_kernel(
    adjoint, viscosity, base, x_one, x_two, y_one, y_two, z_one, after, out
):
    def sides(axis, one, two):
        odd, place = parity(axis) == 1, lax.axis_index(axis)
        has_before = jnp.where(place > 0, 1.0, 0.0)
        has_after = jnp.where(place < lax.axis_size(axis) - 1, 1.0, 0.0)
        return jnp.where(odd, one, two) * has_before, jnp.where(odd, two, one) * has_after

    y_sides = sides("gy", y_one[...], y_two[...])
    x_visc = sides("gx", x_one[5], x_two[5])
    side = jnp.transpose(z_one[4 * PROF : 4 * PROF + 8, :])
    lane = (1 - parity("gz")) * (CZ - 1)
    lanes = lax.broadcasted_iota(jnp.int32, (ROWS, CZ), 1)
    visc = viscosity[...].reshape(ROWS, CZ)
    at_edge = jnp.where(lanes == lane, 0.5 * (visc + side[:, 5:6]), 0.0)
    for f in range(5):
        value = adjoint[f].reshape(ROWS, CZ)
        edge = time_step * (at_edge * (side[:, f : f + 1] - value))
        out[f] = base[f] + edge.reshape(CX, CY, CZ)
        for x, beside, other in zip((0, CX - 1), sides("gx", x_one[f], x_two[f]), x_visc):
            weight = 0.5 * (viscosity[x] + other)
            out[f, x] = out[f, x] + time_step * (weight * (beside - adjoint[f, x]))
        for x in range(CX):
            for row, beside in zip((0, CY - 1), y_sides):
                at = slice(row, row + 1)
                other = beside[5 * CX + x : 5 * CX + x + 1]
                weight = 0.5 * (viscosity[x, at, :] + other)
                here = beside[f * CX + x : f * CX + x + 1] - adjoint[f, x, at, :]
                out[f, x, at, :] = out[f, x, at, :] + time_step * (weight * here)


def wide(matrix):
    high, low = split(matrix)
    return jnp.concatenate([high, low, high], axis=1)


def product(left, right):
    high, low = split(right)
    return dot(left, jnp.concatenate([high, high, low], axis=0))


def join_kernel(first, second, third, fourth, edge, joined):
    for at, block in enumerate((first, second, third, fourth)):
        joined[at * PROF : (at + 1) * PROF, :] = block[0, :PROF, :]
    place = lax.axis_index("gz")
    inner = (place ^ (place >> 1)) & 1 == 1
    nearer = (place >> 2) & 1 == (place >> 1) & 1
    passed = jnp.where(nearer, second[0, PROF:, :], fourth[0, PROF:, :])
    joined[4 * PROF : 4 * PROF + 8, :] = edge[...]
    joined[4 * PROF + 8 :, :] = jnp.where(inner, first[0, PROF:, :], passed)


def solve_kernel(mine, theirs, rows, lift, readout, *refs):
    solved = refs[-1]
    inverse = [
        ref[at * PROF : (at + 1) * PROF, :] for ref in (mine, theirs) for at in range(HALF // 2)
    ]
    read = wide(jnp.concatenate([readout[...], jnp.zeros((3, PROF), F32)], axis=0))
    spread = wide(lift[...])
    inverses = [wide(inverse[p]) for p in range(HALF)]
    folded = [wide(product(read, inverse[p])) for p in range(HALF)]
    rows = [rows[p * 6 : (p + 1) * 6, :] for p in range(HALF)]
    forcing = [product(spread, r) for r in rows]
    damping = [0.5 * r[5:6] for r in rows]
    right = forcing
    for sweep in range(ITERS - 1):
        profile = [product(w, r) for w, r in zip(inverses, right)]
        right = [g - d * jnp.tanh(q) for g, d, q in zip(forcing, damping, profile)]
    for p in range(HALF):
        result = product(folded[p], right[p])
        for f in range(5):
            solved[f * HALF + p : f * HALF + p + 1, :] = result[f : f + 1]
    solved[5 * HALF :, :] = theirs[4 * PROF + 8 :, :]


def scatter_kernel(
    solved_own,
    returned,
    cell,
    patch,
    ranks,
    partial,
    adjoint,
    viscosity,
    updated,
    shear,
):
    parts = (solved_own[: 5 * HALF, :], returned[: 5 * HALF, :])
    result = jnp.concatenate(parts, axis=0)
    rank_hot = one_hot(CAP, ranks[...], BF16)
    back = dot(
        jnp.concatenate(split(result), axis=1), jnp.concatenate([rank_hot, rank_hot], axis=0)
    )
    patches = slot_group(patch[...])
    numbers = lax.broadcasted_iota(jnp.int32, (HALF, FACES), 0)
    kept = [numbers == patches, numbers + HALF == patches]
    walls = []
    for f in range(5):
        parts = [back[at + f * HALF : at + (f + 1) * HALF] for at in (0, 5 * HALF)]
        both = jnp.where(kept[0], parts[0], 0.0) + jnp.where(kept[1], parts[1], 0.0)
        walls.append(jnp.sum(both, axis=0, keepdims=True))
    wall = jnp.concatenate(walls + [jnp.zeros((3, FACES), F32)], axis=0)
    shear[...] = wall[:5]

    side = jnp.transpose(returned[5 * HALF :, :])
    lane = parity("gz") * (CZ - 1)
    lanes = lax.broadcasted_iota(jnp.int32, (ROWS, CZ), 1)
    visc = viscosity[...].reshape(ROWS, CZ)
    at_edge = jnp.where(lanes == lane, 0.5 * (visc + side[:, 5:6]), 0.0)
    cells = cell[...]
    span_hot = one_hot(CZ, cells & (CZ - 1), BF16)
    row_hot = lax.broadcasted_iota(jnp.int32, (ROWS, FACES), 0) == (cells >> 8)
    high = wall.astype(BF16).astype(F32)
    low = wall - high
    for f in range(5):
        spread = [jnp.where(row_hot, part[f : f + 1], 0.0).astype(BF16) for part in (high, low)]
        both = dot_t(jnp.concatenate(spread, axis=0), span_hot)
        source = both[:ROWS] + both[ROWS:]
        value = adjoint[f].reshape(ROWS, CZ)
        edge = at_edge * (side[:, f : f + 1] - value)
        updated[f] = partial[f] + (time_step * (source + edge)).reshape(CX, CY, CZ)


def swapped(array, axis, partner):
    return lax.ppermute(array, axis, [(i, partner(i)) for i in range(lax.axis_size(axis))])


def first_side(array, axis):
    return swapped(array, axis, lambda i: i ^ 1)


def second_side(array, axis):
    size = lax.axis_size(axis)
    return swapped(array, axis, lambda i: (i + 1 if i % 2 else i - 1) % size)


def shape(*dims, dtype=F32):
    return jax.ShapeDtypeStruct(dims, dtype)


def body(
    adjoint, viscosity, flux_jacobian, face_cell, face_patch, wall_inverse, lift_matrix, readout
):
    cell = face_cell.reshape(1, FACES)
    patch = face_patch.reshape(1, FACES)
    face_x, face_y, face_z = shape(6, CY, CZ), shape(6 * CX, CZ), shape(8, ROWS)
    slots, numbers = shape(HALF * 6, CAP), shape(1, FACES, dtype=jnp.int32)
    arrays = [adjoint, viscosity, cell, patch, wall_inverse]
    package = shape(1, PROF + 8, PROF)
    adjoint, viscosity, cell, patch, package, y_one = pl.pallas_call(
        load_kernel,
        out_shape=tuple(shape(*a.shape, dtype=a.dtype) for a in arrays[:4])
        + (package, face_y),
        in_specs=[HBM] * 5,
        out_specs=[VMEM] * 6,
        scratch_shapes=[pltpu.SemaphoreType.DMA((5,))],
        compiler_params=PARAMS,
        name="load",
    )(*[pltpu.with_memory_space_constraint(a, pltpu.HBM) for a in arrays])
    blocks = [package]
    for step in range(1, 4):
        blocks.append(swapped(package, "gz", lambda i: i ^ (4 * step)))
    fields = (adjoint, viscosity, cell, patch)
    gathered = (slots, slots, numbers, face_z)
    y_one = first_side(y_one, "gy")
    y_two, *found = pl.pallas_call(
        early_kernel,
        out_shape=(face_y,) + gathered,
        in_specs=[VMEM] * 4 + [ANY] * 2,
        out_specs=[VMEM] * 5,
        compiler_params=PARAMS,
        name="early_gather",
    )(*fields, y_one, y_one)
    y_two = second_side(y_two, "gy")
    own, other, ranks, z_one = pl.pallas_call(
        late_kernel,
        out_shape=gathered,
        in_specs=[VMEM] * 8,
        out_specs=[VMEM] * 4,
        compiler_params=PARAMS,
        cost_estimate=LONG,
        name="late_gather",
    )(*fields, *found)
    mine = pl.pallas_call(
        join_kernel,
        out_shape=shape(4 * PROF + 16, PROF),
        in_specs=[VMEM] * 5,
        out_specs=VMEM,
        compiler_params=PARAMS,
        name="join",
    )(*blocks, z_one)
    theirs = swapped(mine, "gz", lambda i: i ^ 1)
    base = pl.pallas_call(
        interior,
        out_shape=shape(5, CX, CY, CZ),
        in_specs=[VMEM, VMEM, SMEM, ANY],
        out_specs=VMEM,
        compiler_params=PARAMS,
        cost_estimate=SHORT,
        name="interior",
    )(adjoint, viscosity, flux_jacobian, mine)
    x_one, x_two, other = pl.pallas_call(
        faces_kernel,
        out_shape=(face_x, face_x, slots),
        in_specs=[VMEM, VMEM, VMEM, ANY, ANY],
        out_specs=[VMEM] * 3,
        compiler_params=PARAMS,
        cost_estimate=LONG,
        name="faces",
    )(adjoint, viscosity, other, y_two, base)
    arrived = swapped(other, "gz", lambda i: i ^ 2)
    def solve(rows, *after):
        return pl.pallas_call(
            solve_kernel,
            out_shape=shape(5 * HALF + 8, CAP),
            in_specs=[VMEM] * 5 + [ANY] * len(after),
            out_specs=VMEM,
            compiler_params=PARAMS,
            cost_estimate=LONG,
            name="solve",
        )(mine, theirs, rows, lift_matrix, readout, *after)

    solved_arrived = solve(arrived)
    returned = swapped(solved_arrived, "gz", lambda i: i ^ 2)
    solved_own = solve(own, solved_arrived)
    partial = pl.pallas_call(
        stencil_kernel,
        out_shape=shape(5, CX, CY, CZ),
        in_specs=[VMEM] * 8 + [ANY],
        out_specs=VMEM,
        compiler_params=PARAMS,
        cost_estimate=LONG,
        name="stencil",
    )(
        adjoint,
        viscosity,
        base,
        first_side(x_one, "gx"),
        second_side(x_two, "gx"),
        y_one,
        y_two,
        theirs,
        solved_own,
    )
    return pl.pallas_call(
        scatter_kernel,
        out_shape=(shape(5, CX, CY, CZ), shape(5, FACES)),
        in_specs=[VMEM] * 8,
        out_specs=[VMEM] * 2,
        compiler_params=PARAMS,
        name="scatter",
    )(
        solved_own,
        returned,
        cell,
        patch,
        ranks,
        partial,
        adjoint,
        viscosity,
    )


def solution(mesh):
    in_specs = (
        P(None, "gx", "gy", "gz"),
        P("gx", "gy", "gz"),
        P(),
        P(("gx", "gy", "gz")),
        P(("gx", "gy", "gz"), None),
        P(("gx", "gy", "gz"), None, None),
        P(),
        P(),
    )
    out_specs = (P(None, "gx", "gy", "gz"), P(None, ("gx", "gy", "gz")))
    return jax.shard_map(body, mesh=mesh, in_specs=in_specs, out_specs=out_specs, check_vma=False)
```
